32 devices in a mesh: dp: 32 (over z, y, x, core).
Axes of the slice: x: 2, y: 2, z: 4, core: 2. Of those that a mesh axis runs over, the one named last changes fastest.
Arguments:
- embeddings: float32 [65536, 1024], P('dp'), may hold values from -400 to 400
- start_block: float32 [1024, 256], replicated, may hold values from -6 to 6
Outputs:
- axes_out: float32 [1024, 256], replicated
- scores_out: float32 [65536, 256], P('dp')
The draws below stay inside these ranges and needn't reach their ends.
All inputs are finite; a program needn't handle non-finite values.
Results may differ from the reference program's by a relative error of at most 0.0001.
Values sent between devices are 32-bit elements; how exact they have to be, the bound alone decides.
No kernel may reach another device: no remote copies, remote signals or barrier semaphores. Data moves between devices by JAX's collectives and lax.ppermute only.
A program may use at most 64 MiB of HBM per device.

```python
import math
import jax
import jax.numpy as jnp
from jax import lax

D = 1024
K = 256
ITERS = 2
ROWS = 65536


def draw_embeddings(key, part):
    key = jax.random.fold_in(key, 7)
    key_base, key_rows, key_cols = jax.random.split(key, 3)
    ramp = 1.0 + 2.0 * jnp.arange(ROWS, dtype=jnp.float32) / ROWS
    row_factor = jnp.exp(jax.random.uniform(key_rows, (ROWS, 1), jnp.float32) * math.log(3.0))
    col_factor = jnp.exp(jax.random.uniform(key_cols, (1, D), jnp.float32) * math.log(10.0))
    base = jnp.clip(jax.random.normal(key_base, (ROWS, D), jnp.float32), -4.0, 4.0)
    return (base * col_factor * row_factor * ramp[:, None]).astype(jnp.float32)


def scatter_about(key, shape, width, reach, kind=jnp.bfloat16):
    return jnp.clip(width * jax.random.normal(key, shape, jnp.float32), -reach, reach).astype(kind)


def setup_inputs(seed: int = 0) -> dict:
    streams_of = jax.random.split(jax.random.key(seed), 3)
    embeddings = draw_embeddings(jax.random.fold_in(streams_of[2], 71), 0)
    start_block = scatter_about(streams_of[1], (D, K), 1.0, 6.0, jnp.float32)
    return dict(embeddings=embeddings, start_block=start_block)


def exact_dot(first, second):
    return jnp.dot(first.astype(jnp.float32), second.astype(jnp.float32), precision=lax.Precision.HIGHEST, preferred_element_type=jnp.float32)

def inner_dot(first, second):
    return lax.dot_general(first.astype(jnp.float32), second.astype(jnp.float32), (((0,), (0,)), ((), ())), precision=lax.Precision.HIGHEST, preferred_element_type=jnp.float32)

def factor(gram_matrix):
    lower_factor = jnp.linalg.cholesky(gram_matrix)
    identity = jnp.eye(gram_matrix.shape[0], dtype=jnp.float32)
    return jax.scipy.linalg.solve_triangular(lower_factor, identity, lower=True).T

def reference(embeddings, start_block):
    current_basis = start_block
    left_basis = None
    for iteration in range(ITERS):
        projected = exact_dot(embeddings, current_basis)
        inverse = factor(inner_dot(projected, projected))
        left_basis = exact_dot(projected, inverse)
        summed = inner_dot(embeddings, left_basis)
        cross_gram = inner_dot(summed, summed)
        current_basis = exact_dot(summed, factor(cross_gram))
    return (current_basis * math.sqrt(D), left_basis * math.sqrt(ROWS))
```

```python
import functools
import math

import jax
import jax.numpy as jnp
from jax import lax
from jax.experimental import pallas as pl
from jax.experimental.pallas import tpu as pltpu
from jax.sharding import PartitionSpec as P

ITERS = 2
BLOCK = 32
SUB = 8
LANES = 128
TILE = 256
VMEM_LIMIT = 48 * 1024 * 1024


def dot(left, right, contract=(1, 0)):
    dims = (((contract[0],), (contract[1],)), ((), ()))
    return lax.dot_general(left, right, dims, preferred_element_type=jnp.float32)


def split2(x):
    high = x.astype(jnp.bfloat16)
    return high, (x - high.astype(jnp.float32)).astype(jnp.bfloat16)


def split3(x):
    high = x.astype(jnp.bfloat16)
    rest = x - high.astype(jnp.float32)
    middle = rest.astype(jnp.bfloat16)
    return high, middle, (rest - middle.astype(jnp.float32)).astype(jnp.bfloat16)


def dot3(left, right, contract=(1, 0)):
    left_high, left_low = left
    right_high, right_low = right
    return (
        dot(left_high, right_high, contract)
        + dot(left_high, right_low, contract)
        + dot(left_low, right_high, contract)
    )


def outer6(left, right):
    lh, lm, ll = split3(left)
    rh, rm, rl = split3(right)
    return dot(
        jnp.concatenate([lh, lh, lm, lm, lh, ll], 0),
        jnp.concatenate([rh, rm, rh, rm, rl, rh], 0),
        (0, 0),
    )


def eliminate(first, second):
    lane = lax.broadcasted_iota(jnp.int32, (1, LANES), 1)
    for base in range(0, BLOCK, SUB):
        height = BLOCK - base
        row = lax.broadcasted_iota(jnp.int32, (height, LANES), 0)
        ra, rb = first[base:], second[base:]
        cols = [
            jnp.broadcast_to(ra[:, base + k : base + k + 1], (height, LANES)) for k in range(SUB)
        ]
        for k in range(SUB):
            scale = lax.rsqrt(cols[k][k : k + 1])
            mult = jnp.where(row > k, cols[k] * scale, 0.0)
            here = lane == base + k
            pa = jnp.where(here, scale, ra[k : k + 1] * scale)
            pb = rb[k : k + 1] * scale
            for q in range(k + 1, SUB):
                cols[q] = cols[q] - mult * (cols[q][k : k + 1] * scale)
            ra = jnp.where(here & (row > k), 0.0, ra) - mult * pa
            rb = rb - mult * pb
            ra = jnp.where(row == k, pa, ra)
            rb = jnp.where(row == k, pb, rb)
        first = jnp.concatenate([first[:base], ra], 0) if base else ra
        second = jnp.concatenate([second[:base], rb], 0) if base else rb
    return first, second


def invert_factor(a_ref):
    n = a_ref.shape[0]

    def step(index, carry):
        start = pl.multiple_of(index * BLOCK, BLOCK)
        rows = pltpu.roll(a_ref[pl.ds(start, BLOCK), :], lax.rem(n - start, n), 1)
        done = jnp.concatenate(eliminate(rows[:, :LANES], rows[:, LANES:]), 1)
        lane = lax.broadcasted_iota(jnp.int32, (BLOCK, n), 1)
        row = lax.broadcasted_iota(jnp.int32, (BLOCK, n), 0)
        upper = jnp.where((lane >= BLOCK) & (lane < n - start), done, 0.0)
        done = jnp.where((lane < BLOCK) & (lane > row), 0.0, done)
        done = pltpu.roll(done, start, 1)
        update = outer6(pltpu.roll(upper, start, 1), done)
        col = lax.broadcasted_iota(jnp.int32, (n, n), 1)
        row = lax.broadcasted_iota(jnp.int32, (n, n), 0)
        gone = (row >= start + BLOCK) & (col >= start) & (col < start + BLOCK)
        a_ref[...] = jnp.where(gone, 0.0, a_ref[...]) - update
        a_ref[pl.ds(start, BLOCK), :] = done
        return carry

    lax.fori_loop(0, n // BLOCK, step, 0)
    col = lax.broadcasted_iota(jnp.int32, (n, n), 1)
    row = lax.broadcasted_iota(jnp.int32, (n, n), 0)
    a_ref[...] = jnp.where(col <= row, a_ref[...], 0.0)


def lower_blocks(blocks):
    return [(i, j) for j in range(blocks) for i in range(j, blocks)]


def moments_kernel(me_ref, e_ref, out_ref, sums):
    blocks = e_ref.shape[1] // TILE
    step = pl.program_id(0)

    @pl.when(step == 0)
    def _():
        sums[...] = jnp.zeros_like(sums)

    flipped = [split2(e_ref[:, i * TILE : (i + 1) * TILE].T) for i in range(blocks)]
    for j in range(blocks):
        right = split2(e_ref[:, j * TILE : (j + 1) * TILE])
        for i in range(j, blocks):
            place = lower_blocks(blocks).index((i, j)) * TILE
            sums[place : place + TILE, :] += dot3(flipped[i], right)

    @pl.when(step == pl.num_programs(0) - 1)
    def _():
        pieces, rows, _ = out_ref.shape
        for piece in range(pieces):
            out_ref[piece ^ me_ref[0]] = sums[piece * rows : (piece + 1) * rows, :]


def moments(embeddings, me, pieces):
    rows, columns = embeddings.shape
    blocks = columns // TILE
    packed = TILE * blocks * (blocks + 1) // 2
    step = min(512, rows)
    shape = (pieces, packed // pieces, TILE)
    return pl.pallas_call(
        moments_kernel,
        grid=(rows // step,),
        in_specs=[
            pl.BlockSpec(memory_space=pltpu.SMEM),
            pl.BlockSpec((step, columns), lambda i: (i, 0)),
        ],
        out_specs=pl.BlockSpec(shape, lambda i: (0, 0, 0)),
        out_shape=jax.ShapeDtypeStruct(shape, jnp.float32),
        scratch_shapes=[pltpu.VMEM((packed, TILE), jnp.float32)],
        compiler_params=pltpu.CompilerParams(vmem_limit_bytes=VMEM_LIMIT),
        name="moments",
    )(me, embeddings)


def exchange(x, flip, devices):
    return lax.ppermute(x, "dp", [(d, d ^ flip) for d in range(devices)])


def phases(bits):
    groups = [[0]] if bits else []
    return groups + [list(range(b, min(b + 2, bits))) for b in range(1, bits, 2)]


def spread(value, group):
    return sum(((value >> place) & 1) << bit for place, bit in enumerate(group))


def sum_over_devices(x, devices, scattered):
    bits = devices.bit_length() - 1
    pieces, rows, columns = x.shape
    for group in phases(scattered):
        size = 1 << len(group)
        x = x.reshape(-1, size, rows, columns)
        mine = x[:, 0]
        others = [exchange(x[:, d], spread(d, group), devices) for d in range(1, size)]
        for other in others:
            mine = mine + other
        x = mine
    x = x.reshape(rows, columns)
    for bit in range(scattered, bits):
        x = x + exchange(x, 1 << bit, devices)
    x = x[None]
    for group in reversed(phases(scattered)):
        size = 1 << len(group)
        parts = [x] + [exchange(x, spread(d, group), devices) for d in range(1, size)]
        x = jnp.stack(parts, 1).reshape(-1, rows, columns)
    return x


def iterate_kernel(me_ref, c_ref, start_ref, axes_ref, weights_ref, packed, c_high, c_low, basis, work, gram, cross):
    pieces, rows, _ = c_ref.shape
    columns, width = start_ref.shape
    blocks = columns // TILE
    for piece in range(pieces):
        packed[piece * rows : (piece + 1) * rows, :] = c_ref[piece ^ me_ref[0]]
    for place, (i, j) in enumerate(lower_blocks(blocks)):
        block = packed[place * TILE : (place + 1) * TILE, :]
        at_i, at_j = pl.ds(i * TILE, TILE), pl.ds(j * TILE, TILE)
        if i == j:
            row = lax.broadcasted_iota(jnp.int32, block.shape, 0)
            col = lax.broadcasted_iota(jnp.int32, block.shape, 1)
            block = jnp.where(row >= col, block, block.T)
        high, low = split2(block)
        c_high[at_i, at_j] = high
        c_low[at_i, at_j] = low
        if i != j:
            high, low = split2(block.T)
            c_high[at_j, at_i] = high
            c_low[at_j, at_i] = low
    basis[...] = start_ref[...]

    def iteration(index, carry):
        current = split2(basis[...])

        def multiply(tile, carry):
            at = pl.ds(pl.multiple_of(tile * TILE, TILE), TILE)
            work[at, :] = dot3((c_high[at, :], c_low[at, :]), current)
            return carry

        lax.fori_loop(0, blocks, multiply, 0)
        gram[...] = dot3(current, split2(work[...]), (0, 0))
        invert_factor(gram)
        inverse = split2(gram[...])
        weights_ref[...] = dot3(current, inverse, (1, 1))
        summed = dot3(split2(work[...]), inverse, (1, 1))
        parts = split2(summed)
        cross[...] = dot3(parts, parts, (0, 0))
        invert_factor(cross)
        basis[...] = dot3(parts, split2(cross[...]), (1, 1))
        return carry

    lax.fori_loop(0, ITERS, iteration, 0)
    axes_ref[...] = basis[...] * math.sqrt(columns)


def iterate(summed, start_block, me):
    columns, width = start_block.shape
    pieces, rows, _ = summed.shape
    whole = jax.ShapeDtypeStruct((columns, width), jnp.float32)
    return pl.pallas_call(
        iterate_kernel,
        in_specs=[
            pl.BlockSpec(memory_space=pltpu.SMEM),
            pl.BlockSpec(memory_space=pltpu.VMEM),
            pl.BlockSpec(memory_space=pltpu.VMEM),
        ],
        out_specs=[pl.BlockSpec(memory_space=pltpu.VMEM)] * 2,
        out_shape=[whole, whole],
        scratch_shapes=[
            pltpu.VMEM((pieces * rows, TILE), jnp.float32),
            pltpu.VMEM((columns, columns), jnp.bfloat16),
            pltpu.VMEM((columns, columns), jnp.bfloat16),
            pltpu.VMEM((columns, width), jnp.float32),
            pltpu.VMEM((columns, width), jnp.float32),
            pltpu.VMEM((width, width), jnp.float32),
            pltpu.VMEM((width, width), jnp.float32),
        ],
        compiler_params=pltpu.CompilerParams(vmem_limit_bytes=VMEM_LIMIT),
        name="iterate",
    )(me, summed, start_block)


def body(embeddings, start_block):
    devices = lax.axis_size("dp")
    rows, columns = embeddings.shape
    blocks = columns // TILE
    packed = TILE * blocks * (blocks + 1) // 2
    bits = devices.bit_length() - 1
    scattered = min(bits, ((packed // 8) & -(packed // 8)).bit_length() - 1)
    pieces = 1 << scattered
    me = (lax.axis_index("dp") % pieces).astype(jnp.int32).reshape(1)
    summed = sum_over_devices(moments(embeddings, me, pieces), devices, scattered)
    axes, weights = iterate(summed, start_block, me)
    scores = jnp.dot(
        embeddings,
        weights * math.sqrt(rows * devices),
        precision=lax.Precision.HIGH,
        preferred_element_type=jnp.float32,
    )
    return axes, scores


def solution(mesh):
    in_specs = (P("dp", None), P())
    out_specs = (P(), P("dp", None))
    return jax.shard_map(body, mesh=mesh, in_specs=in_specs, out_specs=out_specs, check_vma=False)
```

```python
import functools
import math

import jax
import jax.numpy as jnp
from jax import lax
from jax.experimental import pallas as pl
from jax.experimental.pallas import tpu as pltpu
from jax.sharding import PartitionSpec as P

ITERS = 2
BLOCK = 32
SUB = 8
LANES = 128
TILE = 256
HALF = TILE // 2
VMEM_LIMIT = 48 * 1024 * 1024


def dot(left, right, contract=(1, 0)):
    dims = (((contract[0],), (contract[1],)), ((), ()))
    return lax.dot_general(left, right, dims, preferred_element_type=jnp.float32)


def split2(x):
    high = x.astype(jnp.bfloat16)
    return high, (x - high.astype(jnp.float32)).astype(jnp.bfloat16)


def split3(x):
    high = x.astype(jnp.bfloat16)
    rest = x - high.astype(jnp.float32)
    middle = rest.astype(jnp.bfloat16)
    return high, middle, (rest - middle.astype(jnp.float32)).astype(jnp.bfloat16)


def dot3(left, right, contract=(1, 0)):
    left_high, left_low = left
    right_high, right_low = right
    return (
        dot(left_high, right_high, contract)
        + dot(left_high, right_low, contract)
        + dot(left_low, right_high, contract)
    )


def stack_left(x):
    high, middle, low = split3(x)
    return jnp.concatenate([high, high, middle, middle, high, low], 0)


def stack_right(x):
    high, middle, low = split3(x)
    return jnp.concatenate([high, middle, high, middle, low, high], 0)


def self_product(parts):
    high, low = parts
    half = dot(high, high * jnp.bfloat16(0.5), (0, 0)) + dot(high, low, (0, 0))
    return half + half.T


def eliminate(rows, offset):
    lane = lax.broadcasted_iota(jnp.int32, (SUB, LANES), 1)
    row = lax.broadcasted_iota(jnp.int32, (SUB, LANES), 0)
    tiles = BLOCK // SUB
    rows = [list(groups) for groups in rows]
    columns = {}

    def spread_columns(tile):
        for k in range(SUB):
            at = offset + tile * SUB + k
            columns[tile * SUB + k] = {
                i: jnp.broadcast_to(rows[i][0][:, at : at + 1], (SUB, LANES))
                for i in range(tile, tiles)
            }

    spread_columns(0)
    for tile in range(tiles):
        if tile + 1 < tiles:
            spread_columns(tile + 1)
        for k in range(SUB):
            j = tile * SUB + k
            column = columns.pop(j)
            pivot = column[tile][k : k + 1]
            inverse = 1.0 / pivot
            mult = {i: column[i] * inverse for i in range(tile, tiles)}
            for q in range(j + 1, min((tile + 2) * SUB, BLOCK)):
                entry = column[q // SUB][q % SUB : q % SUB + 1]
                for i in range(q // SUB, tiles):
                    columns[q][i] = columns[q][i] - mult[i] * entry
            scale = lax.rsqrt(pivot)
            here = lane == offset + j
            top = [jnp.where(here[:1], 1.0, rows[tile][0][k : k + 1])]
            top += [group[k : k + 1] for group in rows[tile][1:]]
            for i in range(tile, tiles):
                old = rows[i]
                new = [jnp.where(here, 0.0, old[0])] + old[1:]
                new = [x - mult[i] * y for x, y in zip(new, top)]
                if i == tile:
                    kept = [jnp.where(row == k, y * scale, x) for x, y in zip(old, top)]
                    new = [jnp.where(row > k, x, y) for x, y in zip(new, kept)]
                rows[i] = new
    return rows


def invert_factor(a_ref, beside=None):
    n = a_ref.shape[0]
    lane = lax.broadcasted_iota(jnp.int32, (BLOCK, n), 1)
    row = lax.broadcasted_iota(jnp.int32, (BLOCK, n), 0)
    panel = a_ref[0:BLOCK, :]
    for start in range(0, n, BLOCK):
        end = start + BLOCK
        if beside is not None:
            beside(start // BLOCK)
        active = start // LANES
        order = [active] + [g for g in range(n // LANES) if g != active]
        rows = [
            [panel[t : t + SUB, g * LANES : (g + 1) * LANES] for g in order]
            for t in range(0, BLOCK, SUB)
        ]
        rows = eliminate(rows, start % LANES)
        groups = [jnp.concatenate([tile[order.index(g)] for tile in rows], 0) for g in range(n // LANES)]
        upper = jnp.concatenate(groups, 1)
        done = jnp.where((lane < end) & (lane - start > row), 0.0, upper)
        a_ref[start:end, :] = jnp.where(lane < end, done, 0.0)
        if end == n:
            break
        left, right = stack_left(upper), stack_right(done)

        def updated(first, last):
            col = lax.broadcasted_iota(jnp.int32, (last - first, n), 1)
            old = jnp.where((col >= start) & (col < end), 0.0, a_ref[first:last, :])
            return old - dot(left[:, first:last], right, (0, 0))

        panel = updated(end, end + BLOCK)
        if end + BLOCK < n:
            a_ref[end + BLOCK : n, :] = updated(end + BLOCK, n)


def below_diagonal(blocks):
    return [(i, j) for j in range(blocks) for i in range(j + 1, blocks)]


def packed_rows(blocks):
    return TILE * len(below_diagonal(blocks)) + HALF * blocks + HALF * blocks // 2


def moments_kernel(me_ref, e_ref, out_ref, packed, diagonal):
    blocks = e_ref.shape[1] // TILE
    step = pl.program_id(0)

    @pl.when(step == 0)
    def _():
        packed[...] = jnp.zeros_like(packed)
        diagonal[...] = jnp.zeros_like(diagonal)

    parts = [split2(e_ref[:, i * TILE : (i + 1) * TILE]) for i in range(blocks)]
    flipped = [(high.T, low.T) for high, low in parts]
    for j in range(blocks):
        high, low = parts[j]
        diagonal[j] += dot(flipped[j][0], high * jnp.bfloat16(0.5)) + dot(flipped[j][0], low)
    for place, (i, j) in enumerate(below_diagonal(blocks)):
        packed[place * TILE : (place + 1) * TILE, :] += dot3(flipped[i], parts[j])

    @pl.when(step == pl.num_programs(0) - 1)
    def _():
        lower = TILE * len(below_diagonal(blocks))
        corner = lower + HALF * blocks
        for j in range(blocks):
            block = diagonal[j] + diagonal[j].T
            packed[lower + j * HALF : lower + (j + 1) * HALF, :] = block[HALF:]
            at = corner + j // 2 * HALF
            side = j % 2 * HALF
            packed[at : at + HALF, side : side + HALF] = block[:HALF, :HALF]
        pieces, rows, _ = out_ref.shape
        for piece in range(pieces):
            out_ref[piece ^ me_ref[0]] = packed[piece * rows : (piece + 1) * rows, :]


def moments(embeddings, me, pieces):
    rows, columns = embeddings.shape
    blocks = columns // TILE
    packed = packed_rows(blocks)
    step = min(512, rows)
    shape = (pieces, packed // pieces, TILE)
    return pl.pallas_call(
        moments_kernel,
        grid=(rows // step,),
        in_specs=[
            pl.BlockSpec(memory_space=pltpu.SMEM),
            pl.BlockSpec((step, columns), lambda i: (i, 0)),
        ],
        out_specs=pl.BlockSpec(shape, lambda i: (0, 0, 0)),
        out_shape=jax.ShapeDtypeStruct(shape, jnp.float32),
        scratch_shapes=[
            pltpu.VMEM((packed, TILE), jnp.float32),
            pltpu.VMEM((blocks, TILE, TILE), jnp.float32),
        ],
        compiler_params=pltpu.CompilerParams(vmem_limit_bytes=VMEM_LIMIT),
        name="moments",
    )(me, embeddings)


def exchange(x, flip, devices):
    return lax.ppermute(x, "dp", [(d, d ^ flip) for d in range(devices)])


def phases(bits):
    groups = [[0]] if bits else []
    return groups + [list(range(b, min(b + 2, bits))) for b in range(1, bits, 2)]


def spread(value, group):
    return sum(((value >> place) & 1) << bit for place, bit in enumerate(group))


def sum_over_devices(x, devices, scattered):
    bits = devices.bit_length() - 1
    pieces, rows, columns = x.shape
    for group in phases(scattered):
        size = 1 << len(group)
        x = x.reshape(-1, size, rows, columns)
        mine = x[:, 0]
        others = [exchange(x[:, d], spread(d, group), devices) for d in range(1, size)]
        for other in others:
            mine = mine + other
        x = mine
    x = x.reshape(rows, columns)
    for bit in range(scattered, bits):
        x = x + exchange(x, 1 << bit, devices)
    x = x[None]
    for group in reversed(phases(scattered)):
        size = 1 << len(group)
        parts = [x] + [exchange(x, spread(d, group), devices) for d in range(1, size)]
        x = jnp.stack(parts, 1).reshape(-1, rows, columns)
    return x


def iterate_kernel(
    scale, me_ref, c_ref, start_ref, e_ref, axes_ref, scores_ref,
    packed, c_high, c_low, work, gram, cross, rows_in, rows_out, sems,
):
    load = pltpu.make_async_copy(e_ref, rows_in, sems.at[0])
    load.start()
    pieces, rows, _ = c_ref.shape
    columns, width = start_ref.shape
    blocks = columns // TILE
    for piece in range(pieces):
        packed[piece * rows : (piece + 1) * rows, :] = c_ref[piece ^ me_ref[0]]

    def put(i, j, block):
        at_i, at_j = pl.ds(i * TILE, TILE), pl.ds(j * TILE, TILE)
        c_high[at_i, at_j], c_low[at_i, at_j] = split2(block)

    for place, (i, j) in enumerate(below_diagonal(blocks)):
        block = packed[place * TILE : (place + 1) * TILE, :]
        put(i, j, block)
        put(j, i, block.T)
    lower = TILE * len(below_diagonal(blocks))
    corner = lower + HALF * blocks
    for j in range(blocks):
        bottom = packed[lower + j * HALF : lower + (j + 1) * HALF, :]
        at = corner + j // 2 * HALF
        side = j % 2 * HALF
        top = [packed[at : at + HALF, side : side + HALF], bottom[:, :HALF].T]
        put(j, j, jnp.concatenate([jnp.concatenate(top, 1), bottom], 0))

    step_rows = rows_in.shape[0] * BLOCK // width
    basis = start_ref[...]
    for index in range(ITERS):
        current = split2(basis)
        work[...] = dot3((c_high[...], c_low[...]), current)
        product = split2(work[...])
        gram[...] = dot3(current, product, (0, 0))
        invert_factor(gram)
        inverse = split2(gram[...])
        summed = split2(dot3(product, inverse, (1, 1)))
        cross[...] = self_product(summed)
        if index < ITERS - 1:
            invert_factor(cross)
        else:
            weights = split2(dot3(current, inverse, (1, 1)) * scale)
            load.wait()

            def beside(step):
                at = slice(step * step_rows, (step + 1) * step_rows)
                rows_out[at, :] = dot3(split2(rows_in[at, :]), weights)

            invert_factor(cross, beside)
        basis = dot3(summed, split2(cross[...]), (1, 1))
    store = pltpu.make_async_copy(rows_out, scores_ref, sems.at[1])
    store.start()
    axes_ref[...] = basis * math.sqrt(columns)
    store.wait()


def iterate(summed, start_block, embeddings, me, scale):
    columns, width = start_block.shape
    pieces, rows, _ = summed.shape
    count = embeddings.shape[0]
    vmem = pl.BlockSpec(memory_space=pltpu.VMEM)
    anywhere = pl.BlockSpec(memory_space=pl.ANY)
    return pl.pallas_call(
        functools.partial(iterate_kernel, scale),
        in_specs=[pl.BlockSpec(memory_space=pltpu.SMEM), vmem, vmem, anywhere],
        out_specs=[vmem, anywhere],
        out_shape=[
            jax.ShapeDtypeStruct((columns, width), jnp.float32),
            jax.ShapeDtypeStruct((count, width), jnp.float32),
        ],
        scratch_shapes=[
            pltpu.VMEM((pieces * rows, TILE), jnp.float32),
            pltpu.VMEM((columns, columns), jnp.bfloat16),
            pltpu.VMEM((columns, columns), jnp.bfloat16),
            pltpu.VMEM((columns, width), jnp.float32),
            pltpu.VMEM((width, width), jnp.float32),
            pltpu.VMEM((width, width), jnp.float32),
            pltpu.VMEM((count, columns), jnp.float32),
            pltpu.VMEM((count, width), jnp.float32),
            pltpu.SemaphoreType.DMA((2,)),
        ],
        compiler_params=pltpu.CompilerParams(vmem_limit_bytes=VMEM_LIMIT),
        name="iterate",
    )(me, summed, start_block, embeddings)


def body(embeddings, start_block):
    devices = lax.axis_size("dp")
    rows, columns = embeddings.shape
    packed = packed_rows(columns // TILE)
    bits = devices.bit_length() - 1
    scattered = min(bits, ((packed // 8) & -(packed // 8)).bit_length() - 1)
    pieces = 1 << scattered
    me = (lax.axis_index("dp") % pieces).astype(jnp.int32).reshape(1)
    summed = sum_over_devices(moments(embeddings, me, pieces), devices, scattered)
    axes, scores = iterate(summed, start_block, embeddings, me, math.sqrt(rows * devices))
    return axes, scores


def solution(mesh):
    in_specs = (P("dp", None), P())
    out_specs = (P(), P("dp", None))
    return jax.shard_map(body, mesh=mesh, in_specs=in_specs, out_specs=out_specs, check_vma=False)
```

```python
import functools
import math

import jax
import jax.numpy as jnp
from jax import lax
from jax.experimental import pallas as pl
from jax.experimental.pallas import tpu as pltpu
from jax.sharding import PartitionSpec as P

ITERS = 2
BLOCK = 32
SUB = 8
LANES = 128
TILE = 256
HALF = TILE // 2
VMEM_LIMIT = 48 * 1024 * 1024


def dot(left, right, contract=(1, 0)):
    dims = (((contract[0],), (contract[1],)), ((), ()))
    return lax.dot_general(left, right, dims, preferred_element_type=jnp.float32)


def split2(x):
    high = x.astype(jnp.bfloat16)
    return high, (x - high.astype(jnp.float32)).astype(jnp.bfloat16)


def split3(x):
    high = x.astype(jnp.bfloat16)
    rest = x - high.astype(jnp.float32)
    middle = rest.astype(jnp.bfloat16)
    return high, middle, (rest - middle.astype(jnp.float32)).astype(jnp.bfloat16)


def dot3(left, right, contract=(1, 0)):
    left_high, left_low = left
    right_high, right_low = right
    return (
        dot(left_high, right_high, contract)
        + dot(left_high, right_low, contract)
        + dot(left_low, right_high, contract)
    )


def tall3(left, right, contract=(1, 0)):
    tiles = range(0, left[0].shape[0], TILE)
    return jnp.concatenate(
        [dot3([part[t : t + TILE] for part in left], right, contract) for t in tiles], 0
    )


def stack_left(x):
    high, middle, low = split3(x)
    return jnp.concatenate([high, high, middle, middle, high, low], 0)


def stack_right(x):
    high, middle, low = split3(x)
    return jnp.concatenate([high, middle, high, middle, low, high], 0)


def self_product(parts):
    high, low = parts
    half = dot(high, high * jnp.bfloat16(0.5), (0, 0)) + dot(high, low, (0, 0))
    return half + half.T


def eliminate(rows, offset):
    lane = lax.broadcasted_iota(jnp.int32, (SUB, LANES), 1)
    row = lax.broadcasted_iota(jnp.int32, (SUB, LANES), 0)
    tiles = BLOCK // SUB
    rows = [list(groups) for groups in rows]
    columns = {}

    def spread_columns(tile):
        for k in range(SUB):
            at = offset + tile * SUB + k
            columns[tile * SUB + k] = {
                i: jnp.broadcast_to(rows[i][0][:, at : at + 1], (SUB, LANES))
                for i in range(tile, tiles)
            }

    spread_columns(0)
    for tile in range(tiles):
        if tile + 1 < tiles:
            spread_columns(tile + 1)
        for k in range(SUB):
            j = tile * SUB + k
            column = columns.pop(j)
            pivot = column[tile][k : k + 1]
            inverse = 1.0 / pivot
            mult = {i: column[i] * inverse for i in range(tile, tiles)}
            for q in range(j + 1, min((tile + 2) * SUB, BLOCK)):
                entry = column[q // SUB][q % SUB : q % SUB + 1]
                for i in range(q // SUB, tiles):
                    columns[q][i] = columns[q][i] - mult[i] * entry
            scale = lax.rsqrt(pivot)
            here = lane == offset + j
            top = [jnp.where(here[:1], 1.0, rows[tile][0][k : k + 1])]
            top += [group[k : k + 1] for group in rows[tile][1:]]
            for i in range(tile, tiles):
                old = rows[i]
                new = [jnp.where(here, 0.0, old[0])] + old[1:]
                new = [x - mult[i] * y for x, y in zip(new, top)]
                if i == tile:
                    kept = [jnp.where(row == k, y * scale, x) for x, y in zip(old, top)]
                    new = [jnp.where(row > k, x, y) for x, y in zip(new, kept)]
                rows[i] = new
    return rows


def invert_factor(a_ref, beside=None):
    n = a_ref.shape[0]
    lane = lax.broadcasted_iota(jnp.int32, (BLOCK, n), 1)
    row = lax.broadcasted_iota(jnp.int32, (BLOCK, n), 0)
    panel = a_ref[0:BLOCK, :]
    for start in range(0, n, BLOCK):
        end = start + BLOCK
        if beside is not None:
            beside(start // BLOCK)
        active = start // LANES
        order = [active] + [g for g in range(n // LANES) if g != active]
        rows = [
            [panel[t : t + SUB, g * LANES : (g + 1) * LANES] for g in order]
            for t in range(0, BLOCK, SUB)
        ]
        rows = eliminate(rows, start % LANES)
        groups = [jnp.concatenate([tile[order.index(g)] for tile in rows], 0) for g in range(n // LANES)]
        upper = jnp.concatenate(groups, 1)
        done = jnp.where((lane < end) & (lane - start > row), 0.0, upper)
        a_ref[start:end, :] = jnp.where(lane < end, done, 0.0)
        if end == n:
            break
        left, right = stack_left(upper), stack_right(done)

        def updated(first, last):
            col = lax.broadcasted_iota(jnp.int32, (last - first, n), 1)
            old = jnp.where((col >= start) & (col < end), 0.0, a_ref[first:last, :])
            return old - dot(left[:, first:last], right, (0, 0))

        panel = updated(end, end + BLOCK)
        if end + BLOCK < n:
            a_ref[end + BLOCK : n, :] = updated(end + BLOCK, n)


def below_diagonal(blocks):
    return [(i, j) for j in range(blocks) for i in range(j + 1, blocks)]


def packed_rows(blocks):
    return TILE * len(below_diagonal(blocks)) + HALF * blocks + HALF * blocks // 2


def moments_kernel(bounds, me_ref, e_ref, out_ref, rows_in, packed, diagonal, sems):
    blocks = e_ref.shape[1] // TILE
    below = below_diagonal(blocks)
    cuts = list(zip(bounds[:-1], bounds[1:]))
    loads = [
        pltpu.make_async_copy(
            e_ref.at[first:last, :], rows_in.at[first:last, :], sems.at[index]
        )
        for index, (first, last) in enumerate(cuts)
    ]
    for load in loads:
        load.start()
    for index, (first, last) in enumerate(cuts):
        loads[index].wait()
        parts = [split2(rows_in[first:last, i * TILE : (i + 1) * TILE]) for i in range(blocks)]
        flipped = [(high.T, low.T) for high, low in parts]
        for j in range(blocks):
            high, low = parts[j]
            term = dot(flipped[j][0], high * jnp.bfloat16(0.5)) + dot(flipped[j][0], low)
            diagonal[j] = term if index == 0 else diagonal[j] + term
        for place, (i, j) in enumerate(below):
            at = slice(place * TILE, (place + 1) * TILE)
            term = dot3(flipped[i], parts[j])
            packed[at, :] = term if index == 0 else packed[at, :] + term
    lower = TILE * len(below)
    corner = lower + HALF * blocks
    for j in range(blocks):
        block = diagonal[j] + diagonal[j].T
        packed[lower + j * HALF : lower + (j + 1) * HALF, :] = block[HALF:]
        at = corner + j // 2 * HALF
        side = j % 2 * HALF
        packed[at : at + HALF, side : side + HALF] = block[:HALF, :HALF]
    pieces, rows, _ = out_ref.shape
    for piece in range(pieces):
        out_ref[piece ^ me_ref[0]] = packed[piece * rows : (piece + 1) * rows, :]


def moments(embeddings, me, pieces):
    rows, columns = embeddings.shape
    blocks = columns // TILE
    packed = packed_rows(blocks)
    bounds = [0] + [rows // 8 * k for k in (1, 2, 4, 6, 8)]
    shape = (pieces, packed // pieces, TILE)
    return pl.pallas_call(
        functools.partial(moments_kernel, bounds),
        in_specs=[pl.BlockSpec(memory_space=pltpu.SMEM), pl.BlockSpec(memory_space=pl.ANY)],
        out_specs=pl.BlockSpec(memory_space=pltpu.VMEM),
        out_shape=jax.ShapeDtypeStruct(shape, jnp.float32),
        scratch_shapes=[
            pltpu.VMEM((rows, columns), jnp.float32),
            pltpu.VMEM((packed, TILE), jnp.float32),
            pltpu.VMEM((blocks, TILE, TILE), jnp.float32),
            pltpu.SemaphoreType.DMA((len(bounds) - 1,)),
        ],
        compiler_params=pltpu.CompilerParams(vmem_limit_bytes=VMEM_LIMIT),
        name="moments",
    )(me, embeddings)


def exchange(x, flip, devices):
    return lax.ppermute(x, "dp", [(d, d ^ flip) for d in range(devices)])


def phases(bits):
    groups = [[0]] if bits else []
    return groups + [list(range(b, min(b + 2, bits))) for b in range(1, bits, 2)]


def spread(value, group):
    return sum(((value >> place) & 1) << bit for place, bit in enumerate(group))


def sum_over_devices(x, devices, scattered):
    bits = devices.bit_length() - 1
    pieces, rows, columns = x.shape
    for group in phases(scattered):
        size = 1 << len(group)
        x = x.reshape(-1, size, rows, columns)
        mine = x[:, 0]
        others = [exchange(x[:, d], spread(d, group), devices) for d in range(1, size)]
        for other in others:
            mine = mine + other
        x = mine
    x = x.reshape(rows, columns)
    for bit in range(scattered, bits):
        x = x + exchange(x, 1 << bit, devices)
    x = x[None]
    for group in reversed(phases(scattered)):
        size = 1 << len(group)
        parts = [x] + [exchange(x, spread(d, group), devices) for d in range(1, size)]
        x = jnp.stack(parts, 1).reshape(-1, rows, columns)
    return x


def iterate_kernel(
    scale, me_ref, c_ref, start_ref, e_ref, axes_ref, scores_ref,
    packed, c_high, c_low, work, gram, cross, rows_in, rows_out, sems,
):
    load = pltpu.make_async_copy(e_ref, rows_in, sems.at[0])
    first_load = pltpu.make_async_copy(start_ref, work, sems.at[2])
    first_load.start()
    load.start()
    store = pltpu.make_async_copy(rows_out, scores_ref, sems.at[1])
    pieces, rows, _ = c_ref.shape
    columns, width = start_ref.shape
    blocks = columns // TILE
    for piece in range(pieces):
        packed[piece * rows : (piece + 1) * rows, :] = c_ref[piece ^ me_ref[0]]

    def put(i, j, block):
        at_i, at_j = pl.ds(i * TILE, TILE), pl.ds(j * TILE, TILE)
        c_high[at_i, at_j], c_low[at_i, at_j] = split2(block)

    for place, (i, j) in enumerate(below_diagonal(blocks)):
        block = packed[place * TILE : (place + 1) * TILE, :]
        put(i, j, block)
        put(j, i, block.T)
    lower = TILE * len(below_diagonal(blocks))
    corner = lower + HALF * blocks
    for j in range(blocks):
        bottom = packed[lower + j * HALF : lower + (j + 1) * HALF, :]
        at = corner + j // 2 * HALF
        side = j % 2 * HALF
        top = [packed[at : at + HALF, side : side + HALF], bottom[:, :HALF].T]
        put(j, j, jnp.concatenate([jnp.concatenate(top, 1), bottom], 0))

    step_rows = rows_in.shape[0] * BLOCK // width
    first_load.wait()
    basis = work[...]
    for index in range(ITERS):
        current = split2(basis)
        for t in range(0, columns, TILE):
            at = slice(t, t + TILE)
            work[at, :] = dot3((c_high[at, :], c_low[at, :]), current)
        product = split2(work[...])
        gram[...] = dot3(current, product, (0, 0))
        invert_factor(gram)
        inverse = split2(gram[...])
        summed = split2(tall3(product, inverse, (1, 1)))
        cross[...] = self_product(summed)
        if index < ITERS - 1:
            invert_factor(cross)
        else:
            weights = split2(tall3(current, inverse, (1, 1)) * scale)
            load.wait()

            def beside(step):
                at = slice(step * step_rows, (step + 1) * step_rows)
                rows_out[at, :] = dot3(split2(rows_in[at, :]), weights)

            invert_factor(cross, beside)
        if index == ITERS - 1:
            store.start()
        basis = tall3(summed, split2(cross[...]), (1, 1))
    axes_ref[...] = basis * math.sqrt(columns)
    store.wait()


def iterate(summed, start_block, embeddings, me, scale):
    columns, width = start_block.shape
    pieces, rows, _ = summed.shape
    count = embeddings.shape[0]
    vmem = pl.BlockSpec(memory_space=pltpu.VMEM)
    anywhere = pl.BlockSpec(memory_space=pl.ANY)
    return pl.pallas_call(
        functools.partial(iterate_kernel, scale),
        in_specs=[pl.BlockSpec(memory_space=pltpu.SMEM), vmem, anywhere, anywhere],
        out_specs=[vmem, anywhere],
        out_shape=[
            jax.ShapeDtypeStruct((columns, width), jnp.float32),
            jax.ShapeDtypeStruct((count, width), jnp.float32),
        ],
        scratch_shapes=[
            pltpu.VMEM((pieces * rows, TILE), jnp.float32),
            pltpu.VMEM((columns, columns), jnp.bfloat16),
            pltpu.VMEM((columns, columns), jnp.bfloat16),
            pltpu.VMEM((columns, width), jnp.float32),
            pltpu.VMEM((width, width), jnp.float32),
            pltpu.VMEM((width, width), jnp.float32),
            pltpu.VMEM((count, columns), jnp.float32),
            pltpu.VMEM((count, width), jnp.float32),
            pltpu.SemaphoreType.DMA((3,)),
        ],
        compiler_params=pltpu.CompilerParams(vmem_limit_bytes=VMEM_LIMIT),
        name="iterate",
    )(me, summed, start_block, embeddings)


def body(embeddings, start_block):
    devices = lax.axis_size("dp")
    rows, columns = embeddings.shape
    packed = packed_rows(columns // TILE)
    bits = devices.bit_length() - 1
    scattered = min(bits, ((packed // 8) & -(packed // 8)).bit_length() - 1)
    pieces = 1 << scattered
    me = (lax.axis_index("dp") % pieces).astype(jnp.int32).reshape(1)
    summed = sum_over_devices(moments(embeddings, me, pieces), devices, scattered)
    axes, scores = iterate(summed, start_block, embeddings, me, math.sqrt(rows * devices))
    return axes, scores


def solution(mesh):
    in_specs = (P("dp", None), P())
    out_specs = (P(), P("dp", None))
    return jax.shard_map(body, mesh=mesh, in_specs=in_specs, out_specs=out_specs, check_vma=False)
```

```python
import functools
import math

import jax
import jax.numpy as jnp
from jax import lax
from jax.experimental import pallas as pl
from jax.experimental.pallas import tpu as pltpu
from jax.sharding import PartitionSpec as P

ITERS = 2
BLOCK = 32
SUB = 8
AHEAD = 2
LANES = 128
TILE = 256
HALF = TILE // 2
VMEM_LIMIT = 48 * 1024 * 1024


def dot(left, right, contract=(1, 0)):
    dims = (((contract[0],), (contract[1],)), ((), ()))
    return lax.dot_general(left, right, dims, preferred_element_type=jnp.float32)


def split2(x):
    high = x.astype(jnp.bfloat16)
    return high, (x - high.astype(jnp.float32)).astype(jnp.bfloat16)


def split3(x):
    high = x.astype(jnp.bfloat16)
    rest = x - high.astype(jnp.float32)
    middle = rest.astype(jnp.bfloat16)
    return high, middle, (rest - middle.astype(jnp.float32)).astype(jnp.bfloat16)


def dot3(left, right, contract=(1, 0)):
    left_high, left_low = left
    right_high, right_low = right
    return (
        dot(left_high, right_high, contract)
        + dot(left_high, right_low, contract)
        + dot(left_low, right_high, contract)
    )


def tall3(left, right, contract=(1, 0)):
    tiles = range(0, left[0].shape[0], TILE)
    return jnp.concatenate(
        [dot3([part[t : t + TILE] for part in left], right, contract) for t in tiles], 0
    )


def stack_left(x):
    high, middle, low = split3(x)
    return jnp.concatenate([high, high, middle, middle, high, low], 0)


def stack_right(x):
    high, middle, low = split3(x)
    return jnp.concatenate([high, middle, high, middle, low, high], 0)


def self_product(parts):
    high, low = parts
    half = dot(high, high * jnp.bfloat16(0.5), (0, 0)) + dot(high, low, (0, 0))
    return half + half.T


def eliminate(rows, offset):
    lane = lax.broadcasted_iota(jnp.int32, (SUB, LANES), 1)
    row = lax.broadcasted_iota(jnp.int32, (SUB, LANES), 0)
    tiles = BLOCK // SUB
    rows = [list(groups) for groups in rows]
    columns = {}

    def spread_columns(tile):
        for k in range(SUB):
            at = offset + tile * SUB + k
            columns[tile * SUB + k] = {
                i: jnp.broadcast_to(rows[i][0][:, at : at + 1], (SUB, LANES))
                for i in range(tile, tiles)
            }

    spread_columns(0)
    for tile in range(tiles):
        first = offset + tile * SUB
        mine = (lane >= first) & (lane < first + SUB)
        unit = (lane - first == row).astype(jnp.float32)
        for i in range(tile, tiles):
            rows[i][0] = jnp.where(mine, unit if i == tile else 0.0, rows[i][0])
        scales = jnp.zeros((SUB, LANES), jnp.float32)
        for k in range(SUB):
            ahead = k >= AHEAD and tile + 1 < tiles
            if k == AHEAD and ahead:
                spread_columns(tile + 1)
            j = tile * SUB + k
            column = columns.pop(j)
            pivot = column[tile][k : k + 1]
            inverse = 1.0 / pivot
            mult = {i: column[i] * inverse for i in range(tile, tiles)}
            for q in range(j + 1, (tile + (2 if ahead else 1)) * SUB):
                entry = column[q // SUB][q % SUB : q % SUB + 1]
                for i in range(q // SUB, tiles):
                    columns[q][i] = columns[q][i] - mult[i] * entry
            scales = jnp.where(row == k, lax.rsqrt(pivot), scales)
            mult[tile] = jnp.where(row > k, mult[tile], 0.0)
            top = [x[k : k + 1] for x in rows[tile]]
            for i in range(tile, tiles):
                rows[i] = [x - mult[i] * y for x, y in zip(rows[i], top)]
        rows[tile] = [x * scales for x in rows[tile]]
    for tile in range(tiles - 1):
        right = (lane >= offset + (tile + 1) * SUB) & (lane < offset + BLOCK)
        rows[tile][0] = jnp.where(right, 0.0, rows[tile][0])
    return rows


def invert_factor(a_ref, beside=None):
    n = a_ref.shape[0]
    groups = range(n // LANES)
    lane = lax.broadcasted_iota(jnp.int32, (1, LANES), 1)

    def at(group):
        return slice(group * LANES, (group + 1) * LANES)

    panel = [a_ref[0:BLOCK, at(g)] for g in groups]
    for start in range(0, n, BLOCK):
        end = start + BLOCK
        if beside is not None:
            beside(start // BLOCK)
        active, offset = start // LANES, start % LANES
        order = [active] + [g for g in groups if g != active]
        rows = [[panel[g][t : t + SUB] for g in order] for t in range(0, BLOCK, SUB)]
        rows = eliminate(rows, offset)
        done = [jnp.concatenate([tile[order.index(g)] for tile in rows], 0) for g in groups]
        for g in groups:
            kept = done[g] if g < active else jnp.zeros((BLOCK, LANES), jnp.float32)
            if g == active:
                kept = jnp.where(lane < offset + BLOCK, done[g], 0.0)
            a_ref[start:end, at(g)] = kept
        if end == n:
            break
        left, right = (stack(jnp.concatenate(done, 1)) for stack in (stack_left, stack_right))
        gone = (lane >= offset) & (lane < offset + BLOCK)

        def updated(first, last):
            change = dot(left[:, first:last], right, (0, 0))
            old = [a_ref[first:last, at(g)] for g in groups]
            old[active] = jnp.where(gone, 0.0, old[active])
            return [old[g] - change[:, at(g)] for g in groups]

        panel = updated(end, end + BLOCK)
        if end + BLOCK < n:
            for g, value in zip(groups, updated(end + BLOCK, n)):
                a_ref[end + BLOCK : n, at(g)] = value


def below_diagonal(blocks):
    return [(i, j) for j in range(blocks) for i in range(j + 1, blocks)]


def packed_rows(blocks):
    return TILE * len(below_diagonal(blocks)) + HALF * blocks + HALF * blocks // 2


def moments_kernel(
    bounds, me_ref, e_ref, start_ref, out_ref, b_high, b_low,
    rows_in, start_in, packed, diagonal, sems,
):
    blocks = e_ref.shape[1] // TILE
    below = below_diagonal(blocks)
    cuts = list(zip(bounds[:-1], bounds[1:]))
    loads = [
        pltpu.make_async_copy(
            e_ref.at[first:last, :], rows_in.at[first:last, :], sems.at[index]
        )
        for index, (first, last) in enumerate(cuts)
    ]
    loads.append(pltpu.make_async_copy(start_ref, start_in, sems.at[len(cuts)]))
    for load in loads:
        load.start()
    for index, (first, last) in enumerate(cuts):
        loads[index].wait()
        parts = [split2(rows_in[first:last, i * TILE : (i + 1) * TILE]) for i in range(blocks)]
        flipped = [(high.T, low.T) for high, low in parts]
        for j in range(blocks):
            high, low = parts[j]
            term = dot(flipped[j][0], high * jnp.bfloat16(0.5)) + dot(flipped[j][0], low)
            diagonal[j] = term if index == 0 else diagonal[j] + term
        for place, (i, j) in enumerate(below):
            at = slice(place * TILE, (place + 1) * TILE)
            term = dot3(flipped[i], parts[j])
            packed[at, :] = term if index == 0 else packed[at, :] + term
    loads[-1].wait()
    b_high[...], b_low[...] = split2(start_in[...])
    lower = TILE * len(below)
    corner = lower + HALF * blocks
    for j in range(blocks):
        block = diagonal[j] + diagonal[j].T
        packed[lower + j * HALF : lower + (j + 1) * HALF, :] = block[HALF:]
        at = corner + j // 2 * HALF
        side = j % 2 * HALF
        packed[at : at + HALF, side : side + HALF] = block[:HALF, :HALF]
    pieces, rows, _ = out_ref.shape
    for piece in range(pieces):
        out_ref[piece ^ me_ref[0]] = packed[piece * rows : (piece + 1) * rows, :]


def moments(embeddings, start_block, me, pieces):
    rows, columns = embeddings.shape
    width = start_block.shape[1]
    blocks = columns // TILE
    packed = packed_rows(blocks)
    bounds = [0] + [rows // 8 * k for k in (1, 2, 4, 6, 8)]
    shape = (pieces, packed // pieces, TILE)
    steps = len(bounds) - 1
    vmem = pl.BlockSpec(memory_space=pltpu.VMEM)
    anywhere = pl.BlockSpec(memory_space=pl.ANY)
    return pl.pallas_call(
        functools.partial(moments_kernel, bounds),
        in_specs=[pl.BlockSpec(memory_space=pltpu.SMEM), anywhere, anywhere],
        out_specs=[vmem, vmem, vmem],
        out_shape=[
            jax.ShapeDtypeStruct(shape, jnp.float32),
            jax.ShapeDtypeStruct((columns, width), jnp.bfloat16),
            jax.ShapeDtypeStruct((columns, width), jnp.bfloat16),
        ],
        scratch_shapes=[
            pltpu.VMEM((rows, columns), jnp.float32),
            pltpu.VMEM((columns, width), jnp.float32),
            pltpu.VMEM((packed, TILE), jnp.float32),
            pltpu.VMEM((blocks, TILE, TILE), jnp.float32),
            pltpu.SemaphoreType.DMA((steps + 1,)),
        ],
        compiler_params=pltpu.CompilerParams(vmem_limit_bytes=VMEM_LIMIT),
        name="moments",
    )(me, embeddings, start_block)


def exchange(x, flip, devices):
    return lax.ppermute(x, "dp", [(d, d ^ flip) for d in range(devices)])


def phases(bits):
    groups = [[0]] if bits else []
    return groups + [list(range(b, min(b + 2, bits))) for b in range(1, bits, 2)]


def spread(value, group):
    return sum(((value >> place) & 1) << bit for place, bit in enumerate(group))


def sum_over_devices(x, devices, scattered):
    bits = devices.bit_length() - 1
    pieces, rows, columns = x.shape
    for group in phases(scattered):
        size = 1 << len(group)
        x = x.reshape(-1, size, rows, columns)
        mine = x[:, 0]
        others = [exchange(x[:, d], spread(d, group), devices) for d in range(1, size)]
        for other in others:
            mine = mine + other
        x = mine
    x = x.reshape(rows, columns)
    for bit in range(scattered, bits):
        x = x + exchange(x, 1 << bit, devices)
    x = x[None]
    for group in reversed(phases(scattered)):
        size = 1 << len(group)
        parts = [x] + [exchange(x, spread(d, group), devices) for d in range(1, size)]
        x = jnp.stack(parts, 1).reshape(-1, rows, columns)
    return x


def iterate_kernel(
    scale, me_ref, c_ref, b_high, b_low, e_ref, axes_ref, scores_ref,
    packed, c_high, c_low, work, gram, cross, rows_in, rows_out, sems,
):
    load = pltpu.make_async_copy(e_ref, rows_in, sems.at[0])
    load.start()
    store = pltpu.make_async_copy(rows_out, scores_ref, sems.at[1])
    pieces, rows, _ = c_ref.shape
    columns, width = b_high.shape
    blocks = columns // TILE
    for piece in range(pieces):
        packed[piece * rows : (piece + 1) * rows, :] = c_ref[piece ^ me_ref[0]]

    def put(i, j, block):
        at_i, at_j = pl.ds(i * TILE, TILE), pl.ds(j * TILE, TILE)
        c_high[at_i, at_j], c_low[at_i, at_j] = split2(block)

    for place, (i, j) in enumerate(below_diagonal(blocks)):
        block = packed[place * TILE : (place + 1) * TILE, :]
        put(i, j, block)
        put(j, i, block.T)
    lower = TILE * len(below_diagonal(blocks))
    corner = lower + HALF * blocks
    for j in range(blocks):
        bottom = packed[lower + j * HALF : lower + (j + 1) * HALF, :]
        at = corner + j // 2 * HALF
        side = j % 2 * HALF
        top = [packed[at : at + HALF, side : side + HALF], bottom[:, :HALF].T]
        put(j, j, jnp.concatenate([jnp.concatenate(top, 1), bottom], 0))

    step_rows = rows_out.shape[0] * BLOCK // width
    for index in range(ITERS):
        current = split2(basis) if index else (b_high[...], b_low[...])
        for t in range(0, columns, TILE):
            at = slice(t, t + TILE)
            work[at, :] = dot3((c_high[at, :], c_low[at, :]), current)
        product = split2(work[...])
        gram[...] = dot3(current, product, (0, 0))
        invert_factor(gram)
        inverse = split2(gram[...])
        summed = split2(tall3(product, inverse, (1, 1)))
        cross[...] = self_product(summed)
        if index < ITERS - 1:
            invert_factor(cross)
        else:
            weights = split2(tall3(current, inverse, (1, 1)) * scale)
            load.wait()

            def beside(step):
                at = slice(step * step_rows, (step + 1) * step_rows)
                rows_out[at, :] = dot3(split2(rows_in[at, :]), weights)

            invert_factor(cross, beside)
        if index == ITERS - 1:
            store.start()
        basis = tall3(summed, split2(cross[...]), (1, 1))
    axes_ref[...] = basis * math.sqrt(columns)
    store.wait()


def iterate(summed, start_parts, embeddings, me, scale):
    columns, width = start_parts[0].shape
    pieces, rows, _ = summed.shape
    count = embeddings.shape[0]
    vmem = pl.BlockSpec(memory_space=pltpu.VMEM)
    anywhere = pl.BlockSpec(memory_space=pl.ANY)
    return pl.pallas_call(
        functools.partial(iterate_kernel, scale),
        in_specs=[pl.BlockSpec(memory_space=pltpu.SMEM)] + [vmem] * 3 + [anywhere],
        out_specs=[vmem, anywhere],
        out_shape=[
            jax.ShapeDtypeStruct((columns, width), jnp.float32),
            jax.ShapeDtypeStruct((count, width), jnp.float32),
        ],
        scratch_shapes=[
            pltpu.VMEM((pieces * rows, TILE), jnp.float32),
            pltpu.VMEM((columns, columns), jnp.bfloat16),
            pltpu.VMEM((columns, columns), jnp.bfloat16),
            pltpu.VMEM((columns, width), jnp.float32),
            pltpu.VMEM((width, width), jnp.float32),
            pltpu.VMEM((width, width), jnp.float32),
            pltpu.VMEM((count, columns), jnp.float32),
            pltpu.VMEM((count, width), jnp.float32),
            pltpu.SemaphoreType.DMA((2,)),
        ],
        compiler_params=pltpu.CompilerParams(vmem_limit_bytes=VMEM_LIMIT),
        name="iterate",
    )(me, summed, *start_parts, embeddings)


def body(embeddings, start_block):
    devices = lax.axis_size("dp")
    rows, columns = embeddings.shape
    packed = packed_rows(columns // TILE)
    bits = devices.bit_length() - 1
    scattered = min(bits, ((packed // 8) & -(packed // 8)).bit_length() - 1)
    pieces = 1 << scattered
    me = (lax.axis_index("dp") % pieces).astype(jnp.int32).reshape(1)
    local, b_high, b_low = moments(embeddings, start_block, me, pieces)
    summed = sum_over_devices(local, devices, scattered)
    scale = math.sqrt(rows * devices)
    axes, scores = iterate(summed, (b_high, b_low), embeddings, me, scale)
    return axes, scores


def solution(mesh):
    in_specs = (P("dp", None), P())
    out_specs = (P(), P("dp", None))
    return jax.shard_map(body, mesh=mesh, in_specs=in_specs, out_specs=out_specs, check_vma=False)
```

```python
import functools
import math

import jax
import jax.numpy as jnp
from jax import lax
from jax.experimental import pallas as pl
from jax.experimental.pallas import tpu as pltpu
from jax.sharding import PartitionSpec as P

ITERS = 2
BLOCK = 32
SUB = 8
AHEAD = 2
LANES = 128
TILE = 256
HALF = TILE // 2
VMEM_LIMIT = 48 * 1024 * 1024


def dot(left, right, contract=(1, 0)):
    dims = (((contract[0],), (contract[1],)), ((), ()))
    return lax.dot_general(left, right, dims, preferred_element_type=jnp.float32)


def split2(x):
    high = x.astype(jnp.bfloat16)
    return high, (x - high.astype(jnp.float32)).astype(jnp.bfloat16)


def split3(x):
    high = x.astype(jnp.bfloat16)
    rest = x - high.astype(jnp.float32)
    middle = rest.astype(jnp.bfloat16)
    return high, middle, (rest - middle.astype(jnp.float32)).astype(jnp.bfloat16)


def dot3(left, right, contract=(1, 0)):
    left_high, left_low = left
    right_high, right_low = right
    return (
        dot(left_high, right_high, contract)
        + dot(left_high, right_low, contract)
        + dot(left_low, right_high, contract)
    )


def tall3(left, right, contract=(1, 0)):
    tiles = range(0, left[0].shape[0], TILE)
    return jnp.concatenate(
        [dot3([part[t : t + TILE] for part in left], right, contract) for t in tiles], 0
    )


def stack_left(x):
    high, middle, low = split3(x)
    return jnp.concatenate([high, high, middle, middle, high, low], 0)


def stack_right(x):
    high, middle, low = split3(x)
    return jnp.concatenate([high, middle, high, middle, low, high], 0)


def self_product(parts):
    high, low = parts
    half = dot(high, high * jnp.bfloat16(0.5), (0, 0)) + dot(high, low, (0, 0))
    return half + half.T


def eliminate(rows, offset):
    lane = lax.broadcasted_iota(jnp.int32, (SUB, LANES), 1)
    row = lax.broadcasted_iota(jnp.int32, (SUB, LANES), 0)
    tiles = BLOCK // SUB
    rows = [list(groups) for groups in rows]
    columns = {}

    def spread_columns(tile):
        for k in range(SUB):
            at = offset + tile * SUB + k
            columns[tile * SUB + k] = {
                i: jnp.broadcast_to(rows[i][0][:, at : at + 1], (SUB, LANES))
                for i in range(tile, tiles)
            }

    spread_columns(0)
    for tile in range(tiles):
        first = offset + tile * SUB
        mine = (lane >= first) & (lane < first + SUB)
        unit = (lane - first == row).astype(jnp.float32)
        for i in range(tile, tiles):
            rows[i][0] = jnp.where(mine, unit if i == tile else 0.0, rows[i][0])
        scales = jnp.zeros((SUB, LANES), jnp.float32)
        for k in range(SUB):
            ahead = k >= AHEAD and tile + 1 < tiles
            if k == AHEAD and ahead:
                spread_columns(tile + 1)
            j = tile * SUB + k
            column = columns.pop(j)
            pivot = column[tile][k : k + 1]
            inverse = 1.0 / pivot
            mult = {i: column[i] * inverse for i in range(tile, tiles)}
            for q in range(j + 1, (tile + (2 if ahead else 1)) * SUB):
                entry = column[q // SUB][q % SUB : q % SUB + 1]
                for i in range(q // SUB, tiles):
                    columns[q][i] = columns[q][i] - mult[i] * entry
            scales = jnp.where(row == k, lax.rsqrt(pivot), scales)
            mult[tile] = jnp.where(row > k, mult[tile], 0.0)
            top = [x[k : k + 1] for x in rows[tile]]
            for i in range(tile, tiles):
                rows[i] = [x - mult[i] * y for x, y in zip(rows[i], top)]
        rows[tile] = [x * scales for x in rows[tile]]
    for tile in range(tiles - 1):
        right = (lane >= offset + (tile + 1) * SUB) & (lane < offset + BLOCK)
        rows[tile][0] = jnp.where(right, 0.0, rows[tile][0])
    return rows


def invert_factor(a_ref, beside=None):
    n = a_ref.shape[0]
    groups = range(n // LANES)
    lane = lax.broadcasted_iota(jnp.int32, (1, LANES), 1)

    def at(group):
        return slice(group * LANES, (group + 1) * LANES)

    panel = [a_ref[0:BLOCK, at(g)] for g in groups]
    for start in range(0, n, BLOCK):
        end = start + BLOCK
        if beside is not None:
            beside(start // BLOCK)
        active, offset = start // LANES, start % LANES
        order = [active] + [g for g in groups if g != active]
        rows = [[panel[g][t : t + SUB] for g in order] for t in range(0, BLOCK, SUB)]
        rows = eliminate(rows, offset)
        done = [jnp.concatenate([tile[order.index(g)] for tile in rows], 0) for g in groups]
        for g in groups:
            kept = done[g] if g < active else jnp.zeros((BLOCK, LANES), jnp.float32)
            if g == active:
                kept = jnp.where(lane < offset + BLOCK, done[g], 0.0)
            a_ref[start:end, at(g)] = kept
        if end == n:
            break
        left, right = (stack(jnp.concatenate(done, 1)) for stack in (stack_left, stack_right))
        gone = (lane >= offset) & (lane < offset + BLOCK)

        def updated(first, last):
            change = dot(left[:, first:last], right, (0, 0))
            old = [a_ref[first:last, at(g)] for g in groups]
            old[active] = jnp.where(gone, 0.0, old[active])
            return [old[g] - change[:, at(g)] for g in groups]

        panel = updated(end, end + BLOCK)
        if end + BLOCK < n:
            for g, value in zip(groups, updated(end + BLOCK, n)):
                a_ref[end + BLOCK : n, at(g)] = value


def below_diagonal(blocks):
    return [(i, j) for j in range(blocks) for i in range(j + 1, blocks)]


def packed_rows(blocks):
    return TILE * len(below_diagonal(blocks)) + HALF * blocks


def moments_kernel(
    bounds, me_ref, e_ref, out_ref, corners, rows_in, packed, diagonal, sems,
):
    blocks = e_ref.shape[1] // TILE
    below = below_diagonal(blocks)
    cuts = list(zip(bounds[:-1], bounds[1:]))
    loads = [
        pltpu.make_async_copy(
            e_ref.at[first:last, :], rows_in.at[first:last, :], sems.at[index]
        )
        for index, (first, last) in enumerate(cuts)
    ]
    for load in loads:
        load.start()
    for index, (first, last) in enumerate(cuts):
        loads[index].wait()
        parts = [split2(rows_in[first:last, i * TILE : (i + 1) * TILE]) for i in range(blocks)]
        flipped = [(high.T, low.T) for high, low in parts]
        for j in range(blocks):
            high, low = parts[j]
            term = dot(flipped[j][0], high * jnp.bfloat16(0.5)) + dot(flipped[j][0], low)
            diagonal[j] = term if index == 0 else diagonal[j] + term
        for place, (i, j) in enumerate(below):
            at = slice(place * TILE, (place + 1) * TILE)
            term = dot3(flipped[i], parts[j])
            packed[at, :] = term if index == 0 else packed[at, :] + term
    lower = TILE * len(below)
    row = lax.broadcasted_iota(jnp.int32, (HALF, HALF), 0)
    col = lax.broadcasted_iota(jnp.int32, (HALF, HALF), 1)
    corners[...] = jnp.zeros_like(corners)
    for j in range(blocks):
        block = diagonal[j] + diagonal[j].T
        at = slice(lower + j * HALF, lower + (j + 1) * HALF)
        packed[at, :HALF] = block[HALF:, :HALF]
        packed[at, HALF:] = jnp.where(row > col, block[:HALF, :HALF], block[HALF:, HALF:])
        corners[j : j + 1, :HALF] = jnp.sum(
            jnp.where(row == col, block[:HALF, :HALF], 0.0), axis=0, keepdims=True
        )
    pieces, rows, _ = out_ref.shape
    for piece in range(pieces):
        out_ref[piece ^ me_ref[0]] = packed[piece * rows : (piece + 1) * rows, :]


def moments(embeddings, me, pieces):
    rows, columns = embeddings.shape
    blocks = columns // TILE
    packed = packed_rows(blocks)
    bounds = [0] + [rows // 8 * k for k in (1, 2, 4, 6, 8)]
    shape = (pieces, packed // pieces, TILE)
    steps = len(bounds) - 1
    vmem = pl.BlockSpec(memory_space=pltpu.VMEM)
    anywhere = pl.BlockSpec(memory_space=pltpu.HBM)
    return pl.pallas_call(
        functools.partial(moments_kernel, bounds),
        in_specs=[pl.BlockSpec(memory_space=pltpu.SMEM), anywhere],
        out_specs=[vmem] * 2,
        out_shape=[
            jax.ShapeDtypeStruct(shape, jnp.float32),
            jax.ShapeDtypeStruct((-(-blocks // SUB) * SUB, TILE), jnp.float32),
        ],
        scratch_shapes=[
            pltpu.VMEM((rows, columns), jnp.float32),
            pltpu.VMEM((packed, TILE), jnp.float32),
            pltpu.VMEM((blocks, TILE, TILE), jnp.float32),
            pltpu.SemaphoreType.DMA((steps,)),
        ],
        compiler_params=pltpu.CompilerParams(vmem_limit_bytes=VMEM_LIMIT),
        name="moments",
    )(me, embeddings)


def exchange(x, flip, devices):
    return lax.ppermute(x, "dp", [(d, d ^ flip) for d in range(devices)])


def phases(bits):
    groups = [[0]] if bits else []
    return groups + [list(range(b, min(b + 2, bits))) for b in range(1, bits, 2)]


def spread(value, group):
    return sum(((value >> place) & 1) << bit for place, bit in enumerate(group))


def pairwise(terms):
    while len(terms) > 1:
        terms = [a + b for a, b in zip(terms[::2], terms[1::2])]
    return terms[0]


def sum_over_devices(x, rider, devices, scattered):
    bits = devices.bit_length() - 1
    _, rows, columns = x.shape
    extra = rider.shape[0]
    for group in phases(scattered):
        size = 1 << len(group)
        x = x.reshape(-1, size, rows, columns)
        count = x.shape[0]
        mine, riders = x[:, 0], [rider]
        for d in range(1, size):
            message = jnp.concatenate([x[:, d].reshape(count * rows, columns), rider], 0)
            message = exchange(message, spread(d, group), devices)
            mine = mine + message[:-extra].reshape(count, rows, columns)
            riders.append(message[-extra:])
        x, rider = mine, pairwise(riders)
    x = x.reshape(rows, columns)
    for bit in range(scattered, bits):
        message = exchange(jnp.concatenate([x, rider], 0), 1 << bit, devices)
        x, rider = x + message[:rows], rider + message[rows:]
    parts = [x[None]]
    for group in reversed(phases(scattered)):
        x = jnp.stack(parts, 1).reshape(-1, rows, columns)
        parts = [x] + [exchange(x, spread(d, group), devices) for d in range(1, 1 << len(group))]
    return parts, rider


def iterate_kernel(
    scale, halves, me_ref, *refs
):
    c_refs = refs[:halves]
    corners, b_high, b_low, e_ref, axes_ref, scores_ref = refs[halves : halves + 6]
    packed, c_high, c_low, work, gram, cross, rows_in, rows_out, sems = refs[halves + 6 :]
    load = pltpu.make_async_copy(e_ref, rows_in, sems.at[0])
    load.start()
    store = pltpu.make_async_copy(rows_out, scores_ref, sems.at[1])
    count, rows, _ = c_refs[0].shape
    columns, width = b_high.shape
    blocks = columns // TILE
    for part, c_ref in enumerate(c_refs):
        for index in range(count):
            piece = (index * halves + part) ^ me_ref[0]
            packed[pl.ds(pl.multiple_of(piece * rows, SUB), rows), :] = c_ref[index]

    def put(i, j, block):
        at_i, at_j = pl.ds(i * TILE, TILE), pl.ds(j * TILE, TILE)
        c_high[at_i, at_j], c_low[at_i, at_j] = split2(block)

    for place, (i, j) in enumerate(below_diagonal(blocks)):
        block = packed[place * TILE : (place + 1) * TILE, :]
        put(i, j, block)
        put(j, i, block.T)
    lower = TILE * len(below_diagonal(blocks))
    row = lax.broadcasted_iota(jnp.int32, (HALF, HALF), 0)
    col = lax.broadcasted_iota(jnp.int32, (HALF, HALF), 1)
    for j in range(blocks):
        at = slice(lower + j * HALF, lower + (j + 1) * HALF)
        quarter, both = packed[at, :HALF], packed[at, HALF:]
        turned = both.T
        first = jnp.where(row > col, both, jnp.where(row == col, corners[j : j + 1, :HALF], turned))
        second = jnp.where(row > col, turned, both)
        block = [[first, quarter.T], [quarter, second]]
        put(j, j, jnp.concatenate([jnp.concatenate(halves, 1) for halves in block], 0))

    step_rows = rows_out.shape[0] * BLOCK // width
    for index in range(ITERS):
        current = split2(basis) if index else (b_high[...], b_low[...])
        for t in range(0, columns, TILE):
            at = slice(t, t + TILE)
            work[at, :] = dot3((c_high[at, :], c_low[at, :]), current)
        product = split2(work[...])
        gram[...] = dot3(current, product, (0, 0))
        invert_factor(gram)
        inverse = split2(gram[...])
        summed = split2(tall3(product, inverse, (1, 1)))
        cross[...] = self_product(summed)
        if index < ITERS - 1:
            invert_factor(cross)
        else:
            weights = split2(tall3(current, inverse, (1, 1)) * scale)
            load.wait()

            def beside(step):
                at = slice(step * step_rows, (step + 1) * step_rows)
                rows_out[at, :] = dot3(split2(rows_in[at, :]), weights)

            invert_factor(cross, beside)
        if index == ITERS - 1:
            store.start()
        basis = tall3(summed, split2(cross[...]), (1, 1))
    axes_ref[...] = basis * math.sqrt(columns)
    store.wait()


def iterate(summed, corners, start_parts, embeddings, me, scale):
    columns, width = start_parts[0].shape
    pieces, rows, _ = summed[0].shape
    count = embeddings.shape[0]
    vmem = pl.BlockSpec(memory_space=pltpu.VMEM)
    anywhere = pl.BlockSpec(memory_space=pltpu.HBM)
    return pl.pallas_call(
        functools.partial(iterate_kernel, scale, len(summed)),
        in_specs=[pl.BlockSpec(memory_space=pltpu.SMEM)] + [vmem] * (len(summed) + 3) + [anywhere],
        out_specs=[vmem, anywhere],
        out_shape=[
            jax.ShapeDtypeStruct((columns, width), jnp.float32),
            jax.ShapeDtypeStruct((count, width), jnp.float32),
        ],
        scratch_shapes=[
            pltpu.VMEM((len(summed) * pieces * rows, TILE), jnp.float32),
            pltpu.VMEM((columns, columns), jnp.bfloat16),
            pltpu.VMEM((columns, columns), jnp.bfloat16),
            pltpu.VMEM((columns, width), jnp.float32),
            pltpu.VMEM((width, width), jnp.float32),
            pltpu.VMEM((width, width), jnp.float32),
            pltpu.VMEM((count, columns), jnp.float32),
            pltpu.VMEM((count, width), jnp.float32),
            pltpu.SemaphoreType.DMA((2,)),
        ],
        compiler_params=pltpu.CompilerParams(vmem_limit_bytes=VMEM_LIMIT),
        name="iterate",
    )(me, *summed, corners, *start_parts, embeddings)


def body(embeddings, start_block):
    devices = lax.axis_size("dp")
    rows, columns = embeddings.shape
    packed = packed_rows(columns // TILE)
    bits = devices.bit_length() - 1
    scattered = min(bits, ((packed // 8) & -(packed // 8)).bit_length() - 1)
    pieces = 1 << scattered
    me = (lax.axis_index("dp") % pieces).astype(jnp.int32).reshape(1)
    local, corners = moments(embeddings, me, pieces)
    summed, corners = sum_over_devices(local, corners, devices, scattered)
    start, corners = lax.optimization_barrier((start_block, corners))
    high = lax.reduce_precision(start, 8, 7)
    start_parts = (high.astype(jnp.bfloat16), (start - high).astype(jnp.bfloat16))
    scale = math.sqrt(rows * devices)
    axes, scores = iterate(summed, corners, start_parts, embeddings, me, scale)
    return axes, scores


def solution(mesh):
    in_specs = (P("dp", None), P())
    out_specs = (P(), P("dp", None))
    return jax.shard_map(body, mesh=mesh, in_specs=in_specs, out_specs=out_specs, check_vma=False)
```

```python
import functools
import math

import jax
import jax.numpy as jnp
from jax import lax
from jax.experimental import pallas as pl
from jax.experimental.pallas import tpu as pltpu
from jax.sharding import PartitionSpec as P

ITERS = 2
BLOCK = 32
SUB = 8
AHEAD = 2
LANES = 128
TILE = 256
HALF = TILE // 2
VMEM_LIMIT = 48 * 1024 * 1024


def dot(left, right, contract=(1, 0)):
    dims = (((contract[0],), (contract[1],)), ((), ()))
    return lax.dot_general(left, right, dims, preferred_element_type=jnp.float32)


def split2(x):
    high = x.astype(jnp.bfloat16)
    return high, (x - high.astype(jnp.float32)).astype(jnp.bfloat16)


def split3(x):
    high = x.astype(jnp.bfloat16)
    rest = x - high.astype(jnp.float32)
    middle = rest.astype(jnp.bfloat16)
    return high, middle, (rest - middle.astype(jnp.float32)).astype(jnp.bfloat16)


def dot3(left, right, contract=(1, 0)):
    left_high, left_low = left
    right_high, right_low = right
    return (
        dot(left_high, right_high, contract)
        + dot(left_high, right_low, contract)
        + dot(left_low, right_high, contract)
    )


def tall3(left, right, contract=(1, 0)):
    tiles = range(0, left[0].shape[0], TILE)
    return jnp.concatenate(
        [dot3([part[t : t + TILE] for part in left], right, contract) for t in tiles], 0
    )


def stack_left(x):
    high, middle, low = split3(x)
    return jnp.concatenate([high, high, middle, middle, high, low], 0)


def stack_right(x):
    high, middle, low = split3(x)
    return jnp.concatenate([high, middle, high, middle, low, high], 0)


def self_product(parts):
    high, low = parts
    half = dot(high, high * jnp.bfloat16(0.5), (0, 0)) + dot(high, low, (0, 0))
    return half + half.T


def eliminate(rows, offset):
    lane = lax.broadcasted_iota(jnp.int32, (SUB, LANES), 1)
    row = lax.broadcasted_iota(jnp.int32, (SUB, LANES), 0)
    tiles = BLOCK // SUB
    rows = [list(groups) for groups in rows]
    columns = {}

    def spread_columns(tile):
        for k in range(SUB):
            at = offset + tile * SUB + k
            columns[tile * SUB + k] = {
                i: jnp.broadcast_to(rows[i][0][:, at : at + 1], (SUB, LANES))
                for i in range(tile, tiles)
            }

    spread_columns(0)
    for tile in range(tiles):
        first = offset + tile * SUB
        mine = (lane >= first) & (lane < first + SUB)
        unit = (lane - first == row).astype(jnp.float32)
        for i in range(tile, tiles):
            rows[i][0] = jnp.where(mine, unit if i == tile else 0.0, rows[i][0])
        scales = jnp.zeros((SUB, LANES), jnp.float32)
        for k in range(SUB):
            ahead = k >= AHEAD and tile + 1 < tiles
            if k == AHEAD and ahead:
                spread_columns(tile + 1)
            j = tile * SUB + k
            column = columns.pop(j)
            pivot = column[tile][k : k + 1]
            inverse = 1.0 / pivot
            mult = {i: column[i] * inverse for i in range(tile, tiles)}
            for q in range(j + 1, (tile + (2 if ahead else 1)) * SUB):
                entry = column[q // SUB][q % SUB : q % SUB + 1]
                for i in range(q // SUB, tiles):
                    columns[q][i] = columns[q][i] - mult[i] * entry
            scales = jnp.where(row == k, lax.rsqrt(pivot), scales)
            mult[tile] = jnp.where(row > k, mult[tile], 0.0)
            top = [x[k : k + 1] for x in rows[tile]]
            for i in range(tile, tiles):
                rows[i] = [x - mult[i] * y for x, y in zip(rows[i], top)]
        rows[tile] = [x * scales for x in rows[tile]]
    for tile in range(tiles - 1):
        right = (lane >= offset + (tile + 1) * SUB) & (lane < offset + BLOCK)
        rows[tile][0] = jnp.where(right, 0.0, rows[tile][0])
    return rows


def invert_factor(a_ref, beside=None):
    n = a_ref.shape[0]
    groups = range(n // LANES)
    lane = lax.broadcasted_iota(jnp.int32, (1, LANES), 1)

    def at(group):
        return slice(group * LANES, (group + 1) * LANES)

    panel = [a_ref[0:BLOCK, at(g)] for g in groups]
    for start in range(0, n, BLOCK):
        end = start + BLOCK
        if beside is not None:
            beside(start // BLOCK)
        active, offset = start // LANES, start % LANES
        order = [active] + [g for g in groups if g != active]
        rows = [[panel[g][t : t + SUB] for g in order] for t in range(0, BLOCK, SUB)]
        rows = eliminate(rows, offset)
        done = [jnp.concatenate([tile[order.index(g)] for tile in rows], 0) for g in groups]
        for g in groups:
            kept = done[g] if g < active else jnp.zeros((BLOCK, LANES), jnp.float32)
            if g == active:
                kept = jnp.where(lane < offset + BLOCK, done[g], 0.0)
            a_ref[start:end, at(g)] = kept
        if end == n:
            break
        left, right = (stack(jnp.concatenate(done, 1)) for stack in (stack_left, stack_right))
        gone = (lane >= offset) & (lane < offset + BLOCK)

        def updated(first, last):
            change = dot(left[:, first:last], right, (0, 0))
            old = [a_ref[first:last, at(g)] for g in groups]
            old[active] = jnp.where(gone, 0.0, old[active])
            return [old[g] - change[:, at(g)] for g in groups]

        panel = updated(end, end + BLOCK)
        if end + BLOCK < n:
            for g, value in zip(groups, updated(end + BLOCK, n)):
                a_ref[end + BLOCK : n, at(g)] = value


def below_diagonal(blocks):
    return [(i, j) for j in range(blocks) for i in range(j + 1, blocks)]


def packed_rows(blocks):
    return TILE * len(below_diagonal(blocks)) + HALF * blocks


def moments_kernel(
    bounds, me_ref, e_ref, keep, send, corners, rows_in, packed, diagonal, sems,
):
    blocks = e_ref.shape[1] // TILE
    below = below_diagonal(blocks)
    cuts = list(zip(bounds[:-1], bounds[1:]))
    loads = [
        pltpu.make_async_copy(
            e_ref.at[first:last, :], rows_in.at[first:last, :], sems.at[index]
        )
        for index, (first, last) in enumerate(cuts)
    ]
    for load in loads:
        load.start()
    for index, (first, last) in enumerate(cuts):
        loads[index].wait()
        parts = [split2(rows_in[first:last, i * TILE : (i + 1) * TILE]) for i in range(blocks)]
        flipped = [(high.T, low.T) for high, low in parts]
        for j in range(blocks):
            high, low = parts[j]
            term = dot(flipped[j][0], high * jnp.bfloat16(0.5)) + dot(flipped[j][0], low)
            diagonal[j] = term if index == 0 else diagonal[j] + term
        for place, (i, j) in enumerate(below):
            at = slice(place * TILE, (place + 1) * TILE)
            term = dot3(flipped[i], parts[j])
            packed[at, :] = term if index == 0 else packed[at, :] + term
    lower = TILE * len(below)
    row = lax.broadcasted_iota(jnp.int32, (HALF, HALF), 0)
    col = lax.broadcasted_iota(jnp.int32, (HALF, HALF), 1)
    corners[...] = jnp.zeros_like(corners)
    for j in range(blocks):
        block = diagonal[j] + diagonal[j].T
        at = slice(lower + j * HALF, lower + (j + 1) * HALF)
        packed[at, :HALF] = block[HALF:, :HALF]
        packed[at, HALF:] = jnp.where(row > col, block[:HALF, :HALF], block[HALF:, HALF:])
        corners[j : j + 1, :HALF] = jnp.sum(
            jnp.where(row == col, block[:HALF, :HALF], 0.0), axis=0, keepdims=True
        )
    count, rows, _ = keep.shape

    def piece(position):
        start = pl.multiple_of((position ^ me_ref[0]) * rows, SUB)
        return packed[pl.ds(start, rows), :]

    for index in range(count):
        keep[index] = piece(2 * index)
        send[index * rows : (index + 1) * rows, :] = piece(2 * index + 1)
    send[count * rows :, :] = corners[...]


def moments(embeddings, me, pieces):
    rows, columns = embeddings.shape
    blocks = columns // TILE
    packed = packed_rows(blocks)
    bounds = [0] + [rows // 8 * k for k in (1, 2, 4, 6, 8)]
    extra = -(-blocks // SUB) * SUB
    steps = len(bounds) - 1
    vmem = pl.BlockSpec(memory_space=pltpu.VMEM)
    anywhere = pl.BlockSpec(memory_space=pltpu.HBM)
    return pl.pallas_call(
        functools.partial(moments_kernel, bounds),
        in_specs=[pl.BlockSpec(memory_space=pltpu.SMEM), anywhere],
        out_specs=[vmem] * 3,
        out_shape=[
            jax.ShapeDtypeStruct((pieces // 2, packed // pieces, TILE), jnp.float32),
            jax.ShapeDtypeStruct((packed // 2 + extra, TILE), jnp.float32),
            jax.ShapeDtypeStruct((extra, TILE), jnp.float32),
        ],
        scratch_shapes=[
            pltpu.VMEM((rows, columns), jnp.float32),
            pltpu.VMEM((packed, TILE), jnp.float32),
            pltpu.VMEM((blocks, TILE, TILE), jnp.float32),
            pltpu.SemaphoreType.DMA((steps,)),
        ],
        compiler_params=pltpu.CompilerParams(vmem_limit_bytes=VMEM_LIMIT),
        name="moments",
    )(me, embeddings)


def exchange(x, flip, devices):
    return lax.ppermute(x, "dp", [(d, d ^ flip) for d in range(devices)])


def phases(bits):
    groups = [[0]] if bits else []
    return groups + [list(range(b, min(b + 2, bits))) for b in range(1, bits, 2)]


def spread(value, group):
    return sum(((value >> place) & 1) << bit for place, bit in enumerate(group))


def pairwise(terms):
    while len(terms) > 1:
        terms = [a + b for a, b in zip(terms[::2], terms[1::2])]
    return terms[0]


def sum_over_devices(keep, send, rider, devices, scattered):
    bits = devices.bit_length() - 1
    _, rows, columns = keep.shape
    extra = rider.shape[0]
    message = exchange(send, 1, devices)
    x = keep + message[:-extra].reshape(keep.shape)
    rider = rider + message[-extra:]
    for group in phases(scattered)[1:]:
        size = 1 << len(group)
        x = x.reshape(-1, size, rows, columns)
        count = x.shape[0]
        mine, riders = x[:, 0], [rider] * size
        for d in reversed(range(1, size)):
            message = jnp.concatenate([x[:, d].reshape(count * rows, columns), rider], 0)
            message = exchange(message, spread(d, group), devices)
            mine = mine + message[:-extra].reshape(count, rows, columns)
            riders[d] = message[-extra:]
        x, rider = mine, pairwise(riders)
    x = x.reshape(rows, columns)
    for bit in range(scattered, bits):
        message = exchange(jnp.concatenate([x, rider], 0), 1 << bit, devices)
        x, rider = x + message[:rows], rider + message[rows:]
    parts = [x[None]]
    for group in reversed(phases(scattered)):
        x = jnp.stack(parts, 1).reshape(-1, rows, columns)
        parts = [x] + [exchange(x, spread(d, group), devices) for d in range(1, 1 << len(group))]
    return parts, rider


def iterate_kernel(
    scale, halves, me_ref, *refs
):
    c_refs = refs[:halves]
    corners, b_high, b_low, e_ref, axes_ref, scores_ref = refs[halves : halves + 6]
    packed, c_high, c_low, work, gram, cross, rows_in, rows_out, sems = refs[halves + 6 :]
    load = pltpu.make_async_copy(e_ref, rows_in, sems.at[0])
    load.start()
    stores = []
    count, rows, _ = c_refs[0].shape
    columns, width = b_high.shape
    blocks = columns // TILE
    for part, c_ref in enumerate(c_refs):
        for index in range(count):
            piece = (index * halves + part) ^ me_ref[0]
            packed[pl.ds(pl.multiple_of(piece * rows, SUB), rows), :] = c_ref[index]

    def put(i, j, block):
        at_i, at_j = pl.ds(i * TILE, TILE), pl.ds(j * TILE, TILE)
        c_high[at_i, at_j], c_low[at_i, at_j] = split2(block)

    for place, (i, j) in enumerate(below_diagonal(blocks)):
        block = packed[place * TILE : (place + 1) * TILE, :]
        put(i, j, block)
        put(j, i, block.T)
    lower = TILE * len(below_diagonal(blocks))
    row = lax.broadcasted_iota(jnp.int32, (HALF, HALF), 0)
    col = lax.broadcasted_iota(jnp.int32, (HALF, HALF), 1)
    for j in range(blocks):
        at = slice(lower + j * HALF, lower + (j + 1) * HALF)
        quarter, both = packed[at, :HALF], packed[at, HALF:]
        turned = both.T
        first = jnp.where(row > col, both, jnp.where(row == col, corners[j : j + 1, :HALF], turned))
        second = jnp.where(row > col, turned, both)
        block = [[first, quarter.T], [quarter, second]]
        put(j, j, jnp.concatenate([jnp.concatenate(halves, 1) for halves in block], 0))

    step_rows = rows_out.shape[0] * BLOCK // width
    for index in range(ITERS):
        current = split2(basis) if index else (b_high[...], b_low[...])
        for t in range(0, columns, TILE):
            at = slice(t, t + TILE)
            work[at, :] = dot3((c_high[at, :], c_low[at, :]), current)
        product = split2(work[...])
        gram[...] = dot3(current, product, (0, 0))
        invert_factor(gram)
        inverse = split2(gram[...])
        summed = split2(tall3(product, inverse, (1, 1)))
        cross[...] = self_product(summed)
        if index < ITERS - 1:
            invert_factor(cross)
        else:
            weights = split2(tall3(current, inverse, (1, 1)) * scale)
            load.wait()

            def beside(step):
                at = slice(step * step_rows, (step + 1) * step_rows)
                rows_out[at, :] = dot3(split2(rows_in[at, :]), weights)
                store = pltpu.make_async_copy(
                    rows_out.at[at, :], scores_ref.at[at, :], sems.at[1 + step]
                )
                store.start()
                stores.append(store)

            invert_factor(cross, beside)
        basis = tall3(summed, split2(cross[...]), (1, 1))
    axes_ref[...] = basis * math.sqrt(columns)
    for store in stores:
        store.wait()


def iterate(summed, corners, start_parts, embeddings, me, scale):
    columns, width = start_parts[0].shape
    pieces, rows, _ = summed[0].shape
    count = embeddings.shape[0]
    vmem = pl.BlockSpec(memory_space=pltpu.VMEM)
    anywhere = pl.BlockSpec(memory_space=pltpu.HBM)
    return pl.pallas_call(
        functools.partial(iterate_kernel, scale, len(summed)),
        in_specs=[pl.BlockSpec(memory_space=pltpu.SMEM)] + [vmem] * (len(summed) + 3) + [anywhere],
        out_specs=[vmem, anywhere],
        out_shape=[
            jax.ShapeDtypeStruct((columns, width), jnp.float32),
            jax.ShapeDtypeStruct((count, width), jnp.float32),
        ],
        scratch_shapes=[
            pltpu.VMEM((len(summed) * pieces * rows, TILE), jnp.float32),
            pltpu.VMEM((columns, columns), jnp.bfloat16),
            pltpu.VMEM((columns, columns), jnp.bfloat16),
            pltpu.VMEM((columns, width), jnp.float32),
            pltpu.VMEM((width, width), jnp.float32),
            pltpu.VMEM((width, width), jnp.float32),
            pltpu.VMEM((count, columns), jnp.float32),
            pltpu.VMEM((count, width), jnp.float32),
            pltpu.SemaphoreType.DMA((1 + width // BLOCK,)),
        ],
        compiler_params=pltpu.CompilerParams(vmem_limit_bytes=VMEM_LIMIT),
        name="iterate",
    )(me, *summed, corners, *start_parts, embeddings)


def body(embeddings, start_block):
    devices = lax.axis_size("dp")
    rows, columns = embeddings.shape
    packed = packed_rows(columns // TILE)
    bits = devices.bit_length() - 1
    scattered = min(bits, ((packed // 8) & -(packed // 8)).bit_length() - 1)
    pieces = 1 << scattered
    me = (lax.axis_index("dp") % pieces).astype(jnp.int32).reshape(1)
    keep, send, corners = moments(embeddings, me, pieces)
    summed, corners = sum_over_devices(keep, send, corners, devices, scattered)
    start, corners = lax.optimization_barrier((start_block, corners))
    high = lax.reduce_precision(start, 8, 7)
    start_parts = (high.astype(jnp.bfloat16), (start - high).astype(jnp.bfloat16))
    scale = math.sqrt(rows * devices)
    axes, scores = iterate(summed, corners, start_parts, embeddings, me, scale)
    return axes, scores


def solution(mesh):
    in_specs = (P("dp", None), P())
    out_specs = (P(), P("dp", None))
    return jax.shard_map(body, mesh=mesh, in_specs=in_specs, out_specs=out_specs, check_vma=False)
```

```python
import functools
import math

import jax
import jax.numpy as jnp
from jax import lax
from jax.experimental import pallas as pl
from jax.experimental.pallas import tpu as pltpu
from jax.sharding import PartitionSpec as P

ITERS = 2
BLOCK = 32
SUB = 8
AHEAD = 2
LANES = 128
TILE = 256
HALF = TILE // 2
VMEM_LIMIT = 48 * 1024 * 1024


def dot(left, right, contract=(1, 0)):
    dims = (((contract[0],), (contract[1],)), ((), ()))
    return lax.dot_general(left, right, dims, preferred_element_type=jnp.float32)


def split2(x):
    high = x.astype(jnp.bfloat16)
    return high, (x - high.astype(jnp.float32)).astype(jnp.bfloat16)


def split3(x):
    high = x.astype(jnp.bfloat16)
    rest = x - high.astype(jnp.float32)
    middle = rest.astype(jnp.bfloat16)
    return high, middle, (rest - middle.astype(jnp.float32)).astype(jnp.bfloat16)


def dot3(left, right, contract=(1, 0)):
    left_high, left_low = left
    right_high, right_low = right
    return (
        dot(left_high, right_high, contract)
        + dot(left_high, right_low, contract)
        + dot(left_low, right_high, contract)
    )


def tall3(left, right, contract=(1, 0)):
    tiles = range(0, left[0].shape[0], TILE)
    return jnp.concatenate(
        [dot3([part[t : t + TILE] for part in left], right, contract) for t in tiles], 0
    )


def stack_left(x):
    high, middle, low = split3(x)
    return jnp.concatenate([high, high, middle, middle, high, low], 0)


def stack_right(x):
    high, middle, low = split3(x)
    return jnp.concatenate([high, middle, high, middle, low, high], 0)


def self_product(parts):
    high, low = parts
    half = dot(high, high * jnp.bfloat16(0.5), (0, 0)) + dot(high, low, (0, 0))
    return half + half.T


def eliminate(rows, offset):
    lane = lax.broadcasted_iota(jnp.int32, (SUB, LANES), 1)
    row = lax.broadcasted_iota(jnp.int32, (SUB, LANES), 0)
    tiles = BLOCK // SUB
    rows = [list(groups) for groups in rows]
    columns = {}

    def spread_columns(tile):
        for k in range(SUB):
            at = offset + tile * SUB + k
            columns[tile * SUB + k] = {
                i: jnp.broadcast_to(rows[i][0][:, at : at + 1], (SUB, LANES))
                for i in range(tile, tiles)
            }

    spread_columns(0)
    for tile in range(tiles):
        first = offset + tile * SUB
        mine = (lane >= first) & (lane < first + SUB)
        unit = (lane - first == row).astype(jnp.float32)
        for i in range(tile, tiles):
            rows[i][0] = jnp.where(mine, unit if i == tile else 0.0, rows[i][0])
        scales = jnp.zeros((SUB, LANES), jnp.float32)
        for k in range(SUB):
            ahead = k >= AHEAD and tile + 1 < tiles
            if k == AHEAD and ahead:
                spread_columns(tile + 1)
            j = tile * SUB + k
            column = columns.pop(j)
            pivot = column[tile][k : k + 1]
            inverse = 1.0 / pivot
            mult = {i: column[i] * inverse for i in range(tile, tiles)}
            for q in range(j + 1, (tile + (2 if ahead else 1)) * SUB):
                entry = column[q // SUB][q % SUB : q % SUB + 1]
                for i in range(q // SUB, tiles):
                    columns[q][i] = columns[q][i] - mult[i] * entry
            scales = jnp.where(row == k, lax.rsqrt(pivot), scales)
            mult[tile] = jnp.where(row > k, mult[tile], 0.0)
            top = [x[k : k + 1] for x in rows[tile]]
            for i in range(tile, tiles):
                rows[i] = [x - mult[i] * y for x, y in zip(rows[i], top)]
        rows[tile] = [x * scales for x in rows[tile]]
    for tile in range(tiles - 1):
        right = (lane >= offset + (tile + 1) * SUB) & (lane < offset + BLOCK)
        rows[tile][0] = jnp.where(right, 0.0, rows[tile][0])
    return rows


def invert_factor(a_ref, beside=None):
    n = a_ref.shape[0]
    groups = range(n // LANES)
    lane = lax.broadcasted_iota(jnp.int32, (1, LANES), 1)

    def at(group):
        return slice(group * LANES, (group + 1) * LANES)

    panel = [a_ref[0:BLOCK, at(g)] for g in groups]
    for start in range(0, n, BLOCK):
        end = start + BLOCK
        if beside is not None:
            beside(start // BLOCK)
        active, offset = start // LANES, start % LANES
        order = [active] + [g for g in groups if g != active]
        rows = [[panel[g][t : t + SUB] for g in order] for t in range(0, BLOCK, SUB)]
        rows = eliminate(rows, offset)
        done = [jnp.concatenate([tile[order.index(g)] for tile in rows], 0) for g in groups]
        for g in groups:
            kept = done[g] if g < active else jnp.zeros((BLOCK, LANES), jnp.float32)
            if g == active:
                kept = jnp.where(lane < offset + BLOCK, done[g], 0.0)
            a_ref[start:end, at(g)] = kept
        if end == n:
            break
        left, right = (stack(jnp.concatenate(done, 1)) for stack in (stack_left, stack_right))
        gone = (lane >= offset) & (lane < offset + BLOCK)

        def updated(first, last):
            change = dot(left[:, first:last], right, (0, 0))
            old = [a_ref[first:last, at(g)] for g in groups]
            old[active] = jnp.where(gone, 0.0, old[active])
            return [old[g] - change[:, at(g)] for g in groups]

        panel = updated(end, end + BLOCK)
        if end + BLOCK < n:
            for g, value in zip(groups, updated(end + BLOCK, n)):
                a_ref[end + BLOCK : n, at(g)] = value


def below_diagonal(blocks):
    return [(i, j) for j in range(blocks) for i in range(j + 1, blocks)]


def packed_rows(blocks):
    return TILE * len(below_diagonal(blocks)) + HALF * blocks


def moments_kernel(
    bounds, me_ref, e_ref, keep, send, corners, rows_in, packed, diagonal, sems,
):
    blocks = e_ref.shape[1] // TILE
    below = below_diagonal(blocks)
    cuts = list(zip(bounds[:-1], bounds[1:]))
    loads = [
        pltpu.make_async_copy(
            e_ref.at[first:last, :], rows_in.at[first:last, :], sems.at[index]
        )
        for index, (first, last) in enumerate(cuts)
    ]
    for load in loads:
        load.start()
    for index, (first, last) in enumerate(cuts):
        loads[index].wait()
        parts = [split2(rows_in[first:last, i * TILE : (i + 1) * TILE]) for i in range(blocks)]
        flipped = [(high.T, low.T) for high, low in parts]
        for j in range(blocks):
            high, low = parts[j]
            term = dot(flipped[j][0], high * jnp.bfloat16(0.5)) + dot(flipped[j][0], low)
            diagonal[j] = term if index == 0 else diagonal[j] + term
        for place, (i, j) in enumerate(below):
            at = slice(place * TILE, (place + 1) * TILE)
            term = dot3(flipped[i], parts[j])
            packed[at, :] = term if index == 0 else packed[at, :] + term
    lower = TILE * len(below)
    row = lax.broadcasted_iota(jnp.int32, (HALF, HALF), 0)
    col = lax.broadcasted_iota(jnp.int32, (HALF, HALF), 1)
    corners[...] = jnp.zeros_like(corners)
    for j in range(blocks):
        block = diagonal[j] + diagonal[j].T
        at = slice(lower + j * HALF, lower + (j + 1) * HALF)
        packed[at, :HALF] = block[HALF:, :HALF]
        packed[at, HALF:] = jnp.where(row > col, block[:HALF, :HALF], block[HALF:, HALF:])
        corners[j : j + 1, :HALF] = jnp.sum(
            jnp.where(row == col, block[:HALF, :HALF], 0.0), axis=0, keepdims=True
        )
    count, rows, _ = keep.shape

    def piece(position):
        start = pl.multiple_of((position ^ me_ref[0]) * rows, SUB)
        return packed[pl.ds(start, rows), :]

    for index in range(count):
        keep[index] = piece(2 * index)
        send[index * rows : (index + 1) * rows, :] = piece(2 * index + 1)
    send[count * rows :, :] = corners[...]


def moments(embeddings, me, pieces):
    rows, columns = embeddings.shape
    blocks = columns // TILE
    packed = packed_rows(blocks)
    bounds = [0] + [rows // 8 * k for k in (1, 2, 4, 6, 8)]
    extra = -(-blocks // SUB) * SUB
    steps = len(bounds) - 1
    vmem = pl.BlockSpec(memory_space=pltpu.VMEM)
    anywhere = pl.BlockSpec(memory_space=pltpu.HBM)
    return pl.pallas_call(
        functools.partial(moments_kernel, bounds),
        in_specs=[pl.BlockSpec(memory_space=pltpu.SMEM), anywhere],
        out_specs=[vmem] * 3,
        out_shape=[
            jax.ShapeDtypeStruct((pieces // 2, packed // pieces, TILE), jnp.float32),
            jax.ShapeDtypeStruct((packed // 2 + extra, TILE), jnp.float32),
            jax.ShapeDtypeStruct((extra, TILE), jnp.float32),
        ],
        scratch_shapes=[
            pltpu.VMEM((rows, columns), jnp.float32),
            pltpu.VMEM((packed, TILE), jnp.float32),
            pltpu.VMEM((blocks, TILE, TILE), jnp.float32),
            pltpu.SemaphoreType.DMA((steps,)),
        ],
        compiler_params=pltpu.CompilerParams(vmem_limit_bytes=VMEM_LIMIT),
        name="moments",
    )(me, embeddings)


def exchange(x, flip, devices):
    return lax.ppermute(x, "dp", [(d, d ^ flip) for d in range(devices)])


def phases(bits, width):
    groups = [[0]] if bits else []
    return groups + [list(range(b, min(b + width, bits))) for b in range(1, bits, width)]


def spread(value, group):
    return sum(((value >> place) & 1) << bit for place, bit in enumerate(group))


def pairwise(terms):
    while len(terms) > 1:
        terms = [a + b for a, b in zip(terms[::2], terms[1::2])]
    return terms[0]


def sum_over_devices(keep, send, rider, devices, scattered):
    bits = devices.bit_length() - 1
    _, rows, columns = keep.shape
    extra = rider.shape[0]
    message = exchange(send, 1, devices)
    x = keep + message[:-extra].reshape(keep.shape)
    rider = rider + message[-extra:]
    for group in phases(scattered, 3)[1:]:
        size = 1 << len(group)
        x = x.reshape(-1, size, rows, columns)
        count = x.shape[0]
        mine, riders = x[:, 0], [rider] * size
        for d in reversed(range(1, size)):
            message = jnp.concatenate([x[:, d].reshape(count * rows, columns), rider], 0)
            message = exchange(message, spread(d, group), devices)
            mine = mine + message[:-extra].reshape(count, rows, columns)
            riders[d] = message[-extra:]
        x, rider = mine, pairwise(riders)
    x = x.reshape(rows, columns)
    for bit in range(scattered, bits):
        message = exchange(jnp.concatenate([x, rider], 0), 1 << bit, devices)
        x, rider = x + message[:rows], rider + message[rows:]
    parts = [x[None]]
    for group in reversed(phases(scattered, 2)):
        x = jnp.stack(parts, 1).reshape(-1, rows, columns)
        parts = [x] + [exchange(x, spread(d, group), devices) for d in range(1, 1 << len(group))]
    return parts, rider


def iterate_kernel(
    scale, halves, me_ref, *refs
):
    c_refs = refs[:halves]
    corners, b_high, b_low, e_ref, axes_ref, scores_ref = refs[halves : halves + 6]
    packed, c_high, c_low, work, gram, cross, rows_in, rows_out, sems = refs[halves + 6 :]
    load = pltpu.make_async_copy(e_ref, rows_in, sems.at[0])
    load.start()
    stores = []
    count, rows, _ = c_refs[0].shape
    columns, width = b_high.shape
    blocks = columns // TILE
    for part, c_ref in enumerate(c_refs):
        for index in range(count):
            piece = (index * halves + part) ^ me_ref[0]
            packed[pl.ds(pl.multiple_of(piece * rows, SUB), rows), :] = c_ref[index]

    def put(i, j, block):
        at_i, at_j = pl.ds(i * TILE, TILE), pl.ds(j * TILE, TILE)
        c_high[at_i, at_j], c_low[at_i, at_j] = split2(block)

    for place, (i, j) in enumerate(below_diagonal(blocks)):
        block = packed[place * TILE : (place + 1) * TILE, :]
        put(i, j, block)
        put(j, i, block.T)
    lower = TILE * len(below_diagonal(blocks))
    row = lax.broadcasted_iota(jnp.int32, (HALF, HALF), 0)
    col = lax.broadcasted_iota(jnp.int32, (HALF, HALF), 1)
    for j in range(blocks):
        at = slice(lower + j * HALF, lower + (j + 1) * HALF)
        quarter, both = packed[at, :HALF], packed[at, HALF:]
        turned = both.T
        first = jnp.where(row > col, both, jnp.where(row == col, corners[j : j + 1, :HALF], turned))
        second = jnp.where(row > col, turned, both)
        block = [[first, quarter.T], [quarter, second]]
        put(j, j, jnp.concatenate([jnp.concatenate(halves, 1) for halves in block], 0))

    step_rows = rows_out.shape[0] * BLOCK // width
    for index in range(ITERS):
        current = split2(basis) if index else (b_high[...], b_low[...])
        for t in range(0, columns, TILE):
            at = slice(t, t + TILE)
            work[at, :] = dot3((c_high[at, :], c_low[at, :]), current)
        product = split2(work[...])
        gram[...] = dot3(current, product, (0, 0))
        invert_factor(gram)
        inverse = split2(gram[...])
        summed = split2(tall3(product, inverse, (1, 1)))
        cross[...] = self_product(summed)
        if index < ITERS - 1:
            invert_factor(cross)
        else:
            weights = split2(tall3(current, inverse, (1, 1)) * scale)
            load.wait()

            def beside(step):
                at = slice(step * step_rows, (step + 1) * step_rows)
                rows_out[at, :] = dot3(split2(rows_in[at, :]), weights)
                store = pltpu.make_async_copy(
                    rows_out.at[at, :], scores_ref.at[at, :], sems.at[1 + step]
                )
                store.start()
                stores.append(store)

            invert_factor(cross, beside)
        basis = tall3(summed, split2(cross[...]), (1, 1))
    axes_ref[...] = basis * math.sqrt(columns)
    for store in stores:
        store.wait()


def iterate(summed, corners, start_parts, embeddings, me, scale):
    columns, width = start_parts[0].shape
    pieces, rows, _ = summed[0].shape
    count = embeddings.shape[0]
    vmem = pl.BlockSpec(memory_space=pltpu.VMEM)
    anywhere = pl.BlockSpec(memory_space=pltpu.HBM)
    return pl.pallas_call(
        functools.partial(iterate_kernel, scale, len(summed)),
        in_specs=[pl.BlockSpec(memory_space=pltpu.SMEM)] + [vmem] * (len(summed) + 3) + [anywhere],
        out_specs=[vmem, anywhere],
        out_shape=[
            jax.ShapeDtypeStruct((columns, width), jnp.float32),
            jax.ShapeDtypeStruct((count, width), jnp.float32),
        ],
        scratch_shapes=[
            pltpu.VMEM((len(summed) * pieces * rows, TILE), jnp.float32),
            pltpu.VMEM((columns, columns), jnp.bfloat16),
            pltpu.VMEM((columns, columns), jnp.bfloat16),
            pltpu.VMEM((columns, width), jnp.float32),
            pltpu.VMEM((width, width), jnp.float32),
            pltpu.VMEM((width, width), jnp.float32),
            pltpu.VMEM((count, columns), jnp.float32),
            pltpu.VMEM((count, width), jnp.float32),
            pltpu.SemaphoreType.DMA((1 + width // BLOCK,)),
        ],
        compiler_params=pltpu.CompilerParams(vmem_limit_bytes=VMEM_LIMIT),
        name="iterate",
    )(me, *summed, corners, *start_parts, embeddings)


def body(embeddings, start_block):
    devices = lax.axis_size("dp")
    rows, columns = embeddings.shape
    packed = packed_rows(columns // TILE)
    bits = devices.bit_length() - 1
    scattered = min(bits, ((packed // 8) & -(packed // 8)).bit_length() - 1)
    pieces = 1 << scattered
    me = (lax.axis_index("dp") % pieces).astype(jnp.int32).reshape(1)
    keep, send, corners = moments(embeddings, me, pieces)
    summed, corners = sum_over_devices(keep, send, corners, devices, scattered)
    start, corners = lax.optimization_barrier((start_block, corners))
    high = lax.reduce_precision(start, 8, 7)
    start_parts = (high.astype(jnp.bfloat16), (start - high).astype(jnp.bfloat16))
    scale = math.sqrt(rows * devices)
    axes, scores = iterate(summed, corners, start_parts, embeddings, me, scale)
    return axes, scores


def solution(mesh):
    in_specs = (P("dp", None), P())
    out_specs = (P(), P("dp", None))
    return jax.shard_map(body, mesh=mesh, in_specs=in_specs, out_specs=out_specs, check_vma=False)
```
